256 devices in a mesh: tmpl: 32 (over y, x, core), sta: 8 (over z).
Axes of the slice: x: 4, y: 4, z: 8, core: 2. Of those that a mesh axis runs over, the one named last changes fastest.
Arguments:
- records: bfloat16 [64, 1024, 3, 512], P('sta', 'tmpl'), may hold values from -40 to 40
- templates: bfloat16 [16384, 3, 512], P('tmpl'), may hold values from -40 to 40
- requests: int32 [32, 32, 4], P('tmpl'), may hold values from 0 to 31, as said below
- pair_slot: int32 [16384], P('tmpl'), may hold values from 0 to 127
- pair_template: int32 [16384], P('tmpl'), may hold values from 0 to 31, as said below
- pair_offset: int32 [16384], P('tmpl'), may hold values from 0 to 511
- live_pairs: int32 [32], P('tmpl'), may hold values from 32 to 512, as said below
Outputs:
- stacks: float32 [64, 1024, 512], P('sta', 'tmpl')
The draws below stay inside these ranges and needn't reach their ends.
Inputs may be any that keep to these rules, and one draw needn't show every extreme that they name: `requests`: for each owner and index of tmpl, 4 different local station numbers. `pair_template`: each owner's first 32 pair slots name its 32 templates once each. `live_pairs`: the busiest owner holds 512 live pairs.
All inputs are finite; a program needn't handle non-finite values.
Results may differ from the reference program's by a relative error of at most 0.013.
Values may be sent and summed in bfloat16 or wider, within the bound.
A program may use at most 128 MiB of HBM per device.

```python
import jax
import jax.numpy as jnp
from jax import lax

TL = 512
S_DEV = 32
FETCH = 4
T_DEV = 32
PAIRS_DEV = 512
OWNERS = 32
SLOTS = 128
STATIONS = 1024
NHOP = 64
TEMPLATES = 1024
PAIRS = 16384


def draw_records(key, part):
    key = jax.random.fold_in(key, 11)
    first_key, second_key, third_key = jax.random.split(key, 3)
    shape = (NHOP, STATIONS, 3, TL)
    base = jnp.clip(jax.random.normal(first_key, shape, jnp.float32), -5.0, 5.0)
    station_scale = jnp.exp(jax.random.uniform(second_key, (1, STATIONS, 1, 1), jnp.float32, -1.15, 1.15))
    envelope = jnp.exp(jax.random.uniform(third_key, (NHOP, STATIONS, 1, 1), jnp.float32, -0.7, 0.7))
    return (base * station_scale * envelope).astype(jnp.bfloat16)


def draw_templates(key, part):
    key = jax.random.fold_in(key, 12)
    first_key, second_key = jax.random.split(key, 2)
    shape = (PAIRS, 3, TL)
    base = jnp.clip(jax.random.normal(first_key, shape, jnp.float32), -5.0, 5.0)
    gains = jnp.exp(jax.random.uniform(second_key, (PAIRS, 3, 1), jnp.float32, -1.15, 1.15))
    return (base * gains).astype(jnp.bfloat16)


def draw_requests(key, part):
    key = jax.random.fold_in(key, 13)
    scores = jax.random.randint(key, (OWNERS, OWNERS, S_DEV), 0, 4096) * S_DEV + jnp.arange(S_DEV, dtype=jnp.int32)
    ordering = jnp.argsort(scores, axis=-1, stable=True)
    return ordering[..., :FETCH].astype(jnp.int32)


def draw_pair_template(key, part):
    key = jax.random.fold_in(key, 17)
    first_key, second_key = jax.random.split(key, 2)
    scores = jax.random.randint(first_key, (OWNERS, T_DEV), 0, 4096) * T_DEV + jnp.arange(T_DEV, dtype=jnp.int32)
    leading = jnp.argsort(scores, axis=-1, stable=True).astype(jnp.int32)
    remaining = jax.random.randint(second_key, (OWNERS, PAIRS_DEV - T_DEV), 0, T_DEV).astype(jnp.int32)
    return jnp.concatenate([leading, remaining], axis=1).reshape(PAIRS)


def draw_live_pairs(key, part):
    key = jax.random.fold_in(key, 19)
    first_key, second_key = jax.random.split(key, 2)
    spread = PAIRS_DEV - T_DEV
    drawn = jax.random.randint(first_key, (OWNERS,), 0, spread + 1).astype(jnp.int32)
    counts = T_DEV + drawn * drawn // spread
    busiest = jax.random.randint(second_key, (), 0, OWNERS)
    return jnp.where(jnp.arange(OWNERS, dtype=jnp.int32) == busiest, PAIRS_DEV, counts).astype(jnp.int32)


def plant(values, rng, low, largest):
    index_at = [jax.random.randint(jax.random.fold_in(rng, axis), (), 0, length) for axis, length in enumerate(values.shape)]
    main_axis = values.shape.index(max(values.shape))
    neighbour = index_at[:main_axis] + [(index_at[main_axis] + 1) % values.shape[main_axis]] + index_at[main_axis + 1:]
    return values.at[tuple(index_at)].set(low).at[tuple(neighbour)].set(largest)


def setup_inputs(seed: int = 0) -> dict:
    key_of = jax.random.split(jax.random.key(seed), 8)
    return {
        "records": draw_records(jax.random.fold_in(key_of[7], 71), 0),
        "templates": draw_templates(jax.random.fold_in(key_of[7], 71), 0),
        "requests": draw_requests(jax.random.fold_in(key_of[7], 71), 0),
        "pair_slot": plant(jax.random.randint(key_of[3], (PAIRS,), 0, SLOTS), jax.random.fold_in(key_of[3], 1), 0, SLOTS - 1).astype(jnp.int32),
        "pair_template": draw_pair_template(jax.random.fold_in(key_of[7], 71), 0),
        "pair_offset": plant(jax.random.randint(key_of[5], (PAIRS,), 0, TL), jax.random.fold_in(key_of[5], 1), 0, TL - 1).astype(jnp.int32),
        "live_pairs": draw_live_pairs(jax.random.fold_in(key_of[7], 71), 0),
    }


epsilon = 1e-05

def dft_tables(length):
    full_length = 2 * length
    sample_ids = jnp.arange(full_length, dtype=jnp.int32)[:, None]
    frequency = jnp.arange(length, dtype=jnp.int32)[None, :]
    phases = (sample_ids * frequency % full_length).astype(jnp.float32) * (2.0 * jnp.pi / full_length)
    parity = jnp.where(sample_ids % 2 == 0, 1.0, -1.0).astype(jnp.float32)
    second = jnp.where(frequency == 0, parity, -jnp.sin(phases))
    forward = jnp.concatenate([jnp.cos(phases), second], axis=1).astype(jnp.bfloat16)
    bin_ids = jnp.arange(length, dtype=jnp.int32)[:, None]
    lag_ids = jnp.arange(length, dtype=jnp.int32)[None, :]
    angles = (bin_ids * lag_ids % full_length).astype(jnp.float32) * (2.0 * jnp.pi / full_length)
    alternate = jnp.where(lag_ids % 2 == 0, 1.0, -1.0).astype(jnp.float32)
    cosine_rows = jnp.where(bin_ids == 0, 1.0, 2.0 * jnp.cos(angles)) / full_length
    sine_rows = jnp.where(bin_ids == 0, alternate, -2.0 * jnp.sin(angles)) / full_length
    inverse = jnp.concatenate([cosine_rows, sine_rows], axis=0).astype(jnp.bfloat16)
    return (forward, inverse)

def cross_spectrum(template_spec, station_spec):
    length = template_spec.shape[-1] // 2
    left = template_spec.astype(jnp.float32)
    right = station_spec.astype(jnp.float32)
    left_real, left_imag = (left[..., :length], left[..., length:])
    right_real, right_imag = (right[..., :length], right[..., length:])
    zero_bin = jnp.arange(length) == 0
    paired = left_imag * right_imag
    real_part = left_real * right_real + jnp.where(zero_bin, 0.0, paired)
    imag_part = jnp.where(zero_bin, paired, left_real * right_imag - left_imag * right_real)
    return lax.optimization_barrier(jnp.sum(jnp.concatenate([real_part, imag_part], axis=-1), axis=-2))

def reference(records, templates, requests, pair_slot, pair_template, pair_offset, live_pairs):
    highest = lax.Precision.HIGHEST
    forward, inverse = dft_tables(TL)
    forward_wide = forward.astype(jnp.float32)
    forward_short = forward_wide[:TL]
    inverse_wide = inverse.astype(jnp.float32)
    padding = jnp.zeros((2,) + records.shape[1:], records.dtype)
    hop_rows = jnp.transpose(jnp.concatenate([records, padding], axis=0), (1, 0, 2, 3))
    windows = jnp.concatenate([hop_rows[:, :-1], hop_rows[:, 1:]], axis=-1)
    spectra = jnp.dot(windows.reshape(-1, 2 * TL).astype(jnp.float32), forward_wide, precision=highest)
    spectra = spectra.astype(jnp.bfloat16).reshape(windows.shape)
    squares = lax.optimization_barrier(jnp.sum(jnp.square(windows.astype(jnp.float32)), axis=2))
    sample_ids = jnp.arange(2 * TL, dtype=jnp.int32)[:, None]
    lag_ids = jnp.arange(TL, dtype=jnp.int32)[None, :]
    band_matrix = ((sample_ids >= lag_ids) & (sample_ids < lag_ids + TL)).astype(jnp.float32)
    energy = jnp.dot(squares, band_matrix, precision=highest)
    sources = jnp.arange(OWNERS, dtype=jnp.int32)[None, :, None] * S_DEV
    station_ids = (sources + requests).reshape(OWNERS, SLOTS)
    length_scale = 3.0 * TL
    template_ids = jnp.arange(T_DEV, dtype=jnp.int32)

    def one_owner(inputs):
        wanted, shapes, slot_ids, owners_ids, shifts, live_count = inputs
        template_spec = jnp.dot(shapes.reshape(-1, TL).astype(jnp.float32), forward_short, precision=highest)
        template_spec = template_spec.astype(jnp.bfloat16).reshape(PAIRS_DEV, 3, 2 * TL)
        template_energy = lax.optimization_barrier(jnp.sum(jnp.square(shapes.astype(jnp.float32)), axis=(1, 2)))
        stations = wanted[slot_ids]

        def one_window(window):
            station_spec = spectra[stations, window]
            product = cross_spectrum(template_spec, station_spec).astype(jnp.bfloat16)
            lagged = jnp.dot(product.astype(jnp.float32), inverse_wide, precision=highest)
            station_energy = energy[stations, window]
            denominator = length_scale * jnp.sqrt((station_energy / length_scale + epsilon) * (template_energy[:, None] / length_scale + epsilon))
            return lagged / denominator
        normed = lax.map(one_window, jnp.arange(NHOP + 1, dtype=jnp.int32))
        flattened = jnp.transpose(normed, (1, 0, 2)).reshape(PAIRS_DEV, (NHOP + 1) * TL)
        shifted = jax.vmap(lambda row_data, offset: lax.dynamic_slice_in_dim(row_data, offset, NHOP * TL))(flattened, shifts)
        live_rows = jnp.arange(PAIRS_DEV, dtype=jnp.int32) < live_count
        weights = ((owners_ids[:, None] == template_ids[None, :]) & live_rows[:, None]).astype(jnp.float32)
        summed = jnp.dot(weights.T, shifted, precision=highest)
        counts = lax.optimization_barrier(jnp.sum(weights, axis=0))
        stacked = summed * jnp.sqrt(length_scale / counts)[:, None]
        return stacked.reshape(T_DEV, NHOP, TL)
    stacks = lax.map(one_owner, (station_ids, templates.reshape(OWNERS, PAIRS_DEV, 3, TL), pair_slot.reshape(OWNERS, PAIRS_DEV), pair_template.reshape(OWNERS, PAIRS_DEV), pair_offset.reshape(OWNERS, PAIRS_DEV), live_pairs))
    return jnp.transpose(stacks, (2, 0, 1, 3)).reshape(NHOP, TEMPLATES, TL)
```

```python
import functools

import jax
import jax.numpy as jnp
import numpy as np
from jax import lax
from jax.experimental import pallas as pl
from jax.experimental.pallas import tpu as pltpu
from jax.sharding import PartitionSpec as P

TL = 512
NBINS = 2 * TL
T_DEV = 32
FETCH = 4
SCALE = 3.0 * TL
EPSILON = 1e-05
MESH = pl.DeviceIdType.MESH
PB = 16


def dft_tables():
    n = np.arange(TL)[:, None]
    k = np.arange(TL)[None, :]
    angles = (n * k % NBINS) * (2.0 * np.pi / NBINS)
    parity = np.where(n % 2 == 0, 1.0, -1.0)
    second = np.where(k == 0, parity, -np.sin(angles))
    forward = np.concatenate([np.cos(angles), second], axis=1).astype(jnp.bfloat16)
    alternate = np.where(k % 2 == 0, 1.0, -1.0)
    cosine_rows = np.where(n == 0, 1.0, 2.0 * np.cos(angles)) / NBINS
    sine_rows = np.where(n == 0, alternate, -2.0 * np.sin(angles)) / NBINS
    inverse = np.concatenate([cosine_rows, sine_rows], axis=0).astype(jnp.bfloat16)
    return forward, inverse


FORWARD, INVERSE = dft_tables()

GROUPS = 8
PER = 4
ROWS = FETCH * 24


def split(value):
    high = value.astype(jnp.bfloat16)
    low = (value - high.astype(jnp.float32)).astype(jnp.bfloat16)
    return high, low


def mm(left, right):
    return jnp.dot(left, right, preferred_element_type=jnp.float32)


def exchange_kernel(
    count, depth, rec_ref, ask_ref, tmp_ref, fwd_ref, spec_out, rs_out, t_out,
    rec32, asked, wanted, send, recv, halo_send, halo_recv, parts, part_energy, halo_spec,
    spec, rs, temps,
    ask_send_sem, ask_recv_sem, send_sem, recv_sem, halo_send_sem, halo_recv_sem, local_sem,
):
    me = lax.axis_index("tmpl")
    z = lax.axis_index("sta")
    above = lax.rem(z + 1, depth)
    below = lax.rem(z + depth - 1, depth)

    def ahead(i):
        return lax.rem(me + i, count)

    def behind(i):
        return lax.rem(me + count - i, count)

    barrier = pltpu.get_barrier_semaphore()

    def greet(i, carry):
        pl.semaphore_signal(barrier, inc=1, device_id={"tmpl": ahead(i)}, device_id_type=MESH)
        return carry

    lax.fori_loop(1, count, greet, 0)
    pl.semaphore_signal(barrier, inc=1, device_id={"sta": above}, device_id_type=MESH)
    pl.semaphore_signal(barrier, inc=1, device_id={"sta": below}, device_id_type=MESH)

    def widen(i, carry):
        block = rec_ref[i].astype(jnp.float32)
        for g in range(4):
            rec32[g, pl.ds(pl.multiple_of(i * 32, 32), 32), :] = block[:, g * 128:(g + 1) * 128]
        return carry

    lax.fori_loop(0, 24, widen, 0)
    pl.semaphore_wait(barrier, count + 1)

    def ask_copy(i):
        return pltpu.make_async_remote_copy(
            src_ref=ask_ref.at[ahead(i)], dst_ref=asked.at[i],
            send_sem=ask_send_sem.at[i], recv_sem=ask_recv_sem.at[i],
            device_id={"tmpl": ahead(i)}, device_id_type=MESH,
        )

    def ask_start(i, carry):
        ask_copy(i).start()
        return carry

    lax.fori_loop(1, count, ask_start, 0)
    asked[0] = ask_ref[me]

    lane = lax.broadcasted_iota(jnp.int32, (128, 128), 1)

    def template_block(n, carry):
        first = pl.multiple_of(n * 128, 128)
        pieces = [tmp_ref[c, pl.ds(first, 128), :] for c in range(3)]
        energy = sum(jnp.sum(jnp.square(p.astype(jnp.float32)), axis=1, keepdims=True) for p in pieces)
        factor = lax.rsqrt(energy / SCALE + EPSILON) / SCALE
        for c in range(3):
            found = mm(pieces[c], fwd_ref[...]) * factor
            for g in range(4):
                base = n * 4096 + g * 8
                temps[pl.ds(base + c, 128, stride=32), :] = found[:, g * 128:(g + 1) * 128]
                temps[pl.ds(base + c + 3, 128, stride=32), :] = found[:, TL + g * 128:TL + (g + 1) * 128]
        for g in range(4):
            for row in (6, 7):
                temps[pl.ds(n * 4096 + g * 8 + row, 128, stride=32), :] = jnp.zeros((128, 128), jnp.float32)
        return carry

    def ask_wait(i, carry):
        ask_copy(i).wait()
        return carry

    lax.fori_loop(1, count, ask_wait, 0)
    to_scalar = pltpu.make_async_copy(asked, wanted, local_sem.at[0])
    to_scalar.start()
    to_scalar.wait()

    def gather(i):
        rows = []
        for f in range(FETCH):
            s = wanted[i, 0, f]
            for c in range(3):
                rows.append(
                    jnp.concatenate(
                        [rec32[g, pl.ds(c * 32 + s, 8, stride=96), :] for g in range(4)], axis=1
                    )
                )
        return jnp.concatenate(rows, axis=0).astype(jnp.bfloat16)

    def data_copy(i):
        return pltpu.make_async_remote_copy(
            src_ref=send.at[i], dst_ref=recv.at[i],
            send_sem=send_sem.at[i], recv_sem=recv_sem.at[i],
            device_id={"tmpl": behind(i)}, device_id_type=MESH,
        )

    def data_start(i, carry):
        send[i] = gather(i)
        data_copy(i).start()
        return carry

    lax.fori_loop(1, count, data_start, 0)
    recv[0] = gather(0)

    lax.fori_loop(0, 4, template_block, 0)
    out_t = pltpu.make_async_copy(temps, t_out, local_sem.at[1])
    out_t.start()

    row = lax.broadcasted_iota(jnp.int32, (48, PER * ROWS), 0)
    col = lax.broadcasted_iota(jnp.int32, (48, PER * ROWS), 1)
    pick = (col == (row % 16) * 24 + (row // 16) * 8).astype(jnp.bfloat16)
    sample = lax.broadcasted_iota(jnp.int32, (TL, TL), 0)
    lag = lax.broadcasted_iota(jnp.int32, (TL, TL), 1)
    later = (sample >= lag).astype(jnp.bfloat16)
    earlier = (sample < lag).astype(jnp.bfloat16)
    last = lax.broadcasted_iota(jnp.int32, (8, 128), 0) == 7
    odd = jnp.where(lax.broadcasted_iota(jnp.int32, (8, 128), 1) % 2 == 0, 1.0, -1.0)

    def halo_copy(g):
        return pltpu.make_async_remote_copy(
            src_ref=halo_send.at[g], dst_ref=halo_recv.at[g],
            send_sem=halo_send_sem.at[g], recv_sem=halo_recv_sem.at[g],
            device_id={"sta": below}, device_id_type=MESH,
        )

    def main_part(g, slot):
        for k in range(PER):
            i = g * PER + k

            @pl.when(i > 0)
            def _():
                data_copy(i).wait_recv()

        block = recv[pl.ds(g * PER, PER)].reshape(PER * ROWS, TL)
        halo_send[g] = mm(pick, block).astype(jnp.bfloat16)
        halo_copy(g).start()
        for n in range(4):
            columns = pl.ds(n * 256, 256)
            parts[slot, :, columns] = mm(block, fwd_ref[:, columns])
        squares = jnp.square(block.astype(jnp.float32)).reshape(16, 3, 8, TL)
        squares = (squares[:, 0] + squares[:, 1] + squares[:, 2]).reshape(128, TL)
        high, low = split(squares)
        part_energy[slot, 0] = mm(high, later) + mm(low, later)
        part_energy[slot, 1] = mm(high, earlier) + mm(low, earlier)

    def halo_part(g, slot):
        halo_copy(g).wait_recv()
        block = jnp.where(z == depth - 1, jnp.zeros((48, TL), jnp.bfloat16), halo_recv[g])
        found = mm(block, fwd_ref[...])
        for n in range(8):
            halo_spec[n, 0:48, :] = found[:, n * 128:(n + 1) * 128]
        squares = jnp.square(block.astype(jnp.float32))
        high, low = split(squares[0:16] + squares[16:32] + squares[32:48])
        energy = mm(high, earlier) + mm(low, earlier)
        for n in range(4):
            halo_spec[n, 48:64, :] = energy[:, n * 128:(n + 1) * 128]

        def station(s, carry):
            for c in range(3):
                base = pl.multiple_of(s * 24 + c * 8, 8)
                halves = []
                for n in range(8):
                    now = parts[slot, pl.ds(base, 8), pl.ds(n * 128, 128)]
                    beyond = halo_spec[n, pl.ds(c * 16 + s, 8, stride=0), :]
                    following = jnp.where(last, beyond, pltpu.roll(now, 7, 0))
                    halves.append(now + odd * following)
                real = jnp.concatenate(halves[:4], axis=1)
                imag = jnp.concatenate(halves[4:], axis=1)
                spec[(g * 16 + s) * 3 + c] = jnp.concatenate([real, imag], axis=0).astype(jnp.bfloat16)
            base = pl.multiple_of(s * 8, 8)
            for n in range(4):
                columns = pl.ds(n * 128, 128)
                early = part_energy[slot, 1, pl.ds(base, 8), columns]
                beyond = halo_spec[n, pl.ds(48 + s, 8, stride=0), :]
                early = jnp.where(last, beyond, pltpu.roll(early, 7, 0))
                total = part_energy[slot, 0, pl.ds(base, 8), columns] + early
                rs[g * 16 + s, :, columns] = lax.rsqrt(total / SCALE + EPSILON)
            return carry

        lax.fori_loop(0, 16, station, 0)
        out_copies(g)[0].start()
        out_copies(g)[1].start()

    def out_copies(g):
        a = pl.ds(g * 48, 48)
        b = pl.ds(g * 16, 16)
        return (
            pltpu.make_async_copy(spec.at[a], spec_out.at[a], local_sem.at[2 + g]),
            pltpu.make_async_copy(rs.at[b], rs_out.at[b], local_sem.at[2 + GROUPS + g]),
        )

    main_part(0, 0)

    def turn(g, carry):
        main_part(g, lax.rem(g, 2))
        halo_part(g - 1, lax.rem(g - 1, 2))
        return carry

    lax.fori_loop(1, GROUPS, turn, 0)
    halo_part(GROUPS - 1, (GROUPS - 1) % 2)

    def finish(i, carry):
        data_copy(i).wait_send()
        return carry

    lax.fori_loop(1, count, finish, 0)

    def finish_group(g, carry):
        halo_copy(g).wait_send()
        for copy in out_copies(g):
            copy.wait()
        return carry

    lax.fori_loop(0, GROUPS, finish_group, 0)
    out_t.wait()


def exchange_call(mesh, rec, ask, templates, forward):
    count, depth = mesh.shape["tmpl"], mesh.shape["sta"]
    vmem = pl.BlockSpec(memory_space=pltpu.VMEM)
    hbm = pl.BlockSpec(memory_space=pl.ANY)
    f32, bf16 = jnp.float32, jnp.bfloat16
    slots = count * FETCH
    return pl.pallas_call(
        functools.partial(exchange_kernel, count, depth),
        out_shape=[
            jax.ShapeDtypeStruct((slots * 3, 16, TL), bf16),
            jax.ShapeDtypeStruct((slots, 8, TL), f32),
            jax.ShapeDtypeStruct((512 * 32, 128), f32),
        ],
        in_specs=[vmem] * 4,
        out_specs=[hbm] * 3,
        scratch_shapes=[
            pltpu.VMEM((4, 768, 128), f32),
            pltpu.VMEM((count, 1, 128), jnp.int32),
            pltpu.SMEM((count, 1, 128), jnp.int32),
            pltpu.VMEM((count, ROWS, TL), bf16),
            pltpu.VMEM((count, ROWS, TL), bf16),
            pltpu.VMEM((GROUPS, 48, TL), bf16),
            pltpu.VMEM((GROUPS, 48, TL), bf16),
            pltpu.VMEM((2, PER * ROWS, NBINS), f32),
            pltpu.VMEM((2, 2, 128, TL), f32),
            pltpu.VMEM((8, 64, 128), f32),
            pltpu.VMEM((slots * 3, 16, TL), bf16),
            pltpu.VMEM((slots, 8, TL), f32),
            pltpu.VMEM((512 * 32, 128), f32),
            pltpu.SemaphoreType.DMA((count,)),
            pltpu.SemaphoreType.DMA((count,)),
            pltpu.SemaphoreType.DMA((count,)),
            pltpu.SemaphoreType.DMA((count,)),
            pltpu.SemaphoreType.DMA((GROUPS,)),
            pltpu.SemaphoreType.DMA((GROUPS,)),
            pltpu.SemaphoreType.DMA((2 + 2 * GROUPS,)),
        ],
        compiler_params=pltpu.CompilerParams(
            collective_id=0, has_side_effects=True, vmem_limit_bytes=60 * 2**20
        ),
        name="exchange",
    )(rec, ask, templates, forward)


def pair_kernel(slot_ref, tmpl_ref, off_ref, live_ref, spec_ref, rs_ref, t_ref, inv_ref, pt_ref,
                out_ref, head_ref, acc, x0, x1, y0, y1):
    live = live_ref[0]
    nb = (live + PB - 1) // PB
    acc[...] = jnp.zeros_like(acc)
    y0[...] = jnp.zeros_like(y0)
    y1[...] = jnp.zeros_like(y1)
    lane = lax.broadcasted_iota(jnp.int32, (8, 128), 1)

    first = lane == 0

    def cross(block, x):
        for i in range(0, PB, 2):
            qs = [jnp.minimum(block * PB + i + k, 511) for k in range(2)]
            ss = [slot_ref[q] * 3 for q in qs]
            for g in range(4):
                rr, mm = [], []
                for q, s3 in zip(qs, ss):
                    t = t_ref[q, g]
                    R = M = None
                    for c in range(3):
                        b = spec_ref[s3 + c, :, pl.ds(g * 128, 128)].astype(jnp.float32)
                        br, bm = b[:8], b[8:]
                        ar = jnp.broadcast_to(t[c:c + 1], (8, 128))
                        am = jnp.broadcast_to(t[c + 3:c + 4], (8, 128))
                        cr = ar
                        if g == 0:
                            cr = jnp.where(first, am, ar)
                            am = jnp.where(first, 0.0, am)
                        r = ar * br + am * bm
                        m = cr * bm - am * br
                        R = r if R is None else R + r
                        M = m if M is None else M + m
                    rr.append(R)
                    mm.append(M)
                x[pl.ds(i * 8, 16), pl.ds(g * 128, 128)] = jnp.concatenate(rr, axis=0).astype(jnp.bfloat16)
                x[pl.ds(i * 8, 16), pl.ds(512 + g * 128, 128)] = jnp.concatenate(mm, axis=0).astype(jnp.bfloat16)

    def post(block, y):
        for i in range(PB):
            q = block * PB + i
            qc = jnp.clip(q, 0, 511)
            ok = (q >= 0) & (q < live)
            s = slot_ref[qc]
            j = jnp.where(ok, tmpl_ref[qc], 32)
            o = off_ref[qc]
            fine = o % 128
            low = lane < 128 - fine
            v = y[pl.ds(i * 8, 8), :] * rs_ref[s]
            turned = [pltpu.roll(v[:, g * 128:(g + 1) * 128], 128 - fine, 1) for g in range(4)]
            parts = [jnp.where(low, 0.0, turned[0])]
            for g in range(3):
                parts.append(jnp.where(low, turned[g], turned[g + 1]))
            parts.append(jnp.where(low, turned[3], 0.0))
            base = pl.multiple_of(j * 64 + 24 - 8 * (o // 128), 8)
            acc[pl.ds(base, 40), :] += jnp.concatenate(parts, axis=0)

    def dot(x, y):
        y[...] = jnp.dot(x[...], inv_ref[...], preferred_element_type=jnp.float32)

    def body(b2, _):
        b = b2 * 2
        post(b - 2, y0)
        dot(x1, y1)
        cross(b, x0)
        post(b - 1, y1)
        dot(x0, y0)
        cross(b + 1, x1)
        return 0
    x1[...] = jnp.zeros_like(x1)
    lax.fori_loop(0, (nb + 2 + 1) // 2, body, 0)

    same = (pt_ref[...] == lax.broadcasted_iota(jnp.int32, (32, 512), 0)) & (
        lax.broadcasted_iota(jnp.int32, (32, 512), 1) < live)
    counts = jnp.sum(same.astype(jnp.float32), axis=1, keepdims=True)
    scale = jnp.sqrt(1536.0 / counts)
    for g in range(4):
        lanes = pl.ds(g * 128, 128)
        head_ref[:, lanes] = acc[pl.ds(g * 8, 32, stride=64), :] * scale
        for h in range(8):
            v = acc[pl.ds(32 + g * 8 + h, 32, stride=64), :]
            if h < 7:
                v = v + acc[pl.ds(g * 8 + h + 1, 32, stride=64), :]
            out_ref[h, :, lanes] = v * scale


def pair_call(slot, tmpl, off, live, spec, rs, t, inverse, pt):
    smem = pl.BlockSpec(memory_space=pltpu.SMEM)
    vmem = pl.BlockSpec(memory_space=pltpu.VMEM)
    return pl.pallas_call(
        pair_kernel,
        out_shape=[
            jax.ShapeDtypeStruct((8, T_DEV, TL), jnp.float32),
            jax.ShapeDtypeStruct((T_DEV, TL), jnp.float32),
        ],
        in_specs=[smem] * 4 + [vmem] * 5,
        out_specs=[vmem] * 2,
        scratch_shapes=[
            pltpu.VMEM((33 * 64, 128), jnp.float32),
            pltpu.VMEM((PB * 8, NBINS), jnp.bfloat16),
            pltpu.VMEM((PB * 8, NBINS), jnp.bfloat16),
            pltpu.VMEM((PB * 8, TL), jnp.float32),
            pltpu.VMEM((PB * 8, TL), jnp.float32),
        ],
        compiler_params=pltpu.CompilerParams(vmem_limit_bytes=60 * 2**20),
        name="pairs",
    )(slot, tmpl, off, live, spec, rs, t, inverse, pt)


def shards(mesh, records, templates, requests, pair_slot, pair_template, pair_offset, live_pairs):
    count, depth = mesh.shape["tmpl"], mesh.shape["sta"]
    rec = jnp.transpose(records, (0, 2, 1, 3)).reshape(24, 32, TL)
    ask = jnp.pad(requests.reshape(count, 1, FETCH), ((0, 0), (0, 0), (0, 128 - FETCH)))
    spec, rs, temps = exchange_call(
        mesh, rec, ask, jnp.transpose(templates, (1, 0, 2)), jnp.asarray(FORWARD)
    )
    me = lax.axis_index("tmpl")
    slot = ((pair_slot // FETCH - me) % count) * FETCH + pair_slot % FETCH
    out, head = pair_call(
        slot, pair_template, pair_offset, live_pairs, spec, rs, temps.reshape(512, 4, 8, 128),
        jnp.asarray(INVERSE), pair_template.reshape(1, 512),
    )
    head = lax.ppermute(head, "sta", [(i, i - 1) for i in range(1, depth)])
    return out.at[7].add(head)


def solution(mesh):
    in_specs = (
        P("sta", "tmpl", None, None),
        P("tmpl", None, None),
        P("tmpl", None, None),
        P("tmpl"),
        P("tmpl"),
        P("tmpl"),
        P("tmpl"),
    )
    return jax.shard_map(
        functools.partial(shards, mesh), mesh=mesh, in_specs=in_specs,
        out_specs=P("sta", "tmpl", None), check_vma=False,
    )
```

```python
import functools

import jax
import jax.numpy as jnp
import numpy as np
from jax import lax
from jax.experimental import pallas as pl
from jax.experimental.pallas import tpu as pltpu
from jax.sharding import PartitionSpec as P

TL = 512
NBINS = 2 * TL
T_DEV = 32
FETCH = 4
SCALE = 3.0 * TL
EPSILON = 1e-05
MESH = pl.DeviceIdType.MESH
PB = 16
PAIRS = 512
PLACES = 1024


def dft_tables():
    n = np.arange(TL)[:, None]
    k = np.arange(TL)[None, :]
    angles = (n * k % NBINS) * (2.0 * np.pi / NBINS)
    parity = np.where(n % 2 == 0, 1.0, -1.0)
    second = np.where(k == 0, parity, -np.sin(angles))
    forward = np.concatenate([np.cos(angles), second], axis=1).astype(jnp.bfloat16)
    alternate = np.where(k % 2 == 0, 1.0, -1.0)
    cosine_rows = np.where(n == 0, 1.0, 2.0 * np.cos(angles)) / NBINS
    sine_rows = np.where(n == 0, alternate, -2.0 * np.sin(angles)) / NBINS
    inverse = np.concatenate([cosine_rows, sine_rows], axis=0).astype(jnp.bfloat16)
    return forward, inverse


FORWARD, INVERSE = dft_tables()

GROUPS = 8
PER = 4
ROWS = FETCH * 24


def split(value):
    high = value.astype(jnp.bfloat16)
    low = (value - high.astype(jnp.float32)).astype(jnp.bfloat16)
    return high, low


def mm(left, right):
    return jnp.dot(left, right, preferred_element_type=jnp.float32)


def cross_terms(lane, group, template, station):
    real = imag = None
    for c in range(3):
        rows = station(c).astype(jnp.float32)
        br, bm = rows[:8], rows[8:]
        ar = jnp.broadcast_to(template[c:c + 1], (8, 128))
        am = jnp.broadcast_to(template[c + 3:c + 4], (8, 128))
        cr = ar
        if group == 0:
            cr = jnp.where(lane == 0, am, ar)
            am = jnp.where(lane == 0, 0.0, am)
        r = ar * br + am * bm
        m = cr * bm - am * br
        real = r if real is None else real + r
        imag = m if imag is None else imag + m
    return real, imag


def two_pairs(lane, x, i, templates, stations):
    for g in range(4):
        terms = [cross_terms(lane, g, t(g), functools.partial(s, g)) for t, s in zip(templates, stations)]
        for half in range(2):
            rows = jnp.concatenate([t[half] for t in terms], axis=0).astype(jnp.bfloat16)
            x[pl.ds(i * 8, 16), pl.ds(half * TL + g * 128, 128)] = rows


def place_kernel(slot_ref, live_s, order):
    f32, bf16 = jnp.float32, jnp.bfloat16
    live = live_s[0]
    me = lax.axis_index("tmpl")
    y = me // 8
    pair_row = lax.broadcasted_iota(jnp.int32, (PAIRS, PAIRS), 1)
    pair_col = lax.broadcasted_iota(jnp.int32, (PAIRS, PAIRS), 0)
    source = slot_ref[...] // FETCH
    key_row = lax.rem(source + me, 2) * 4 + lax.rem(source // 8 - y + 4, 4)
    key_row = jnp.where(pair_row[:1] < live, key_row, GROUPS).astype(f32)
    ones = jnp.ones((PAIRS, 128), bf16)
    key_col = mm(jnp.where(pair_row == pair_col, key_row, 0.0).astype(bf16), ones)
    wide = jnp.concatenate([key_col] * 4, axis=1)
    ahead_of = (key_row < wide) | ((key_row == wide) & (pair_row < pair_col))
    rank_col = mm(ahead_of.astype(f32).astype(bf16), ones)
    group_row = lax.broadcasted_iota(jnp.int32, (PAIRS, 128), 1).astype(f32)
    below_count = mm(jnp.ones((8, PAIRS), bf16), (key_col < group_row).astype(f32).astype(bf16))[:1]
    gap = jnp.maximum(32.0 * (2.0 * group_row[:1] - 1.0), 0.0) - below_count
    gap = jnp.where((group_row <= key_col) & (group_row < GROUPS), gap, 0.0)
    place_col = rank_col + jnp.maximum(jnp.max(gap, axis=1, keepdims=True), 0.0)
    place_col = jnp.where(key_col < GROUPS, place_col, 2.0 * PLACES)
    number = lax.broadcasted_iota(jnp.int32, (8, PAIRS), 1)
    row_of = lax.broadcasted_iota(jnp.int32, (8, PAIRS), 0)
    digits = jnp.where(row_of == 0, number // 16, jnp.where(row_of == 1, lax.rem(number, 16), 1))
    digits = digits.astype(f32).astype(bf16)
    for n in range(PLACES // 128):
        here = (place_col == group_row + n * 128.0).astype(f32).astype(bf16)
        found = mm(digits, here)
        order[:, pl.ds(n * 128, 128)] = jnp.where(
            found[2:3] > 0.5, found[0:1] * 16.0 + found[1:2], -1.0
        ).astype(jnp.int32)


def place_call(slot, live):
    vmem = pl.BlockSpec(memory_space=pltpu.VMEM)
    return pl.pallas_call(
        place_kernel,
        out_shape=jax.ShapeDtypeStruct((1, PLACES), jnp.int32),
        in_specs=[vmem, pl.BlockSpec(memory_space=pltpu.SMEM)],
        out_specs=vmem,
        name="places",
    )(slot.reshape(1, PAIRS), live)


def exchange_kernel(
    count, depth, order_s, slot_s, rec_ref, ask_ref, tmp_ref, fwd_ref, inv_ref,
    spec_out, rs_out, t_out, done_out,
    rec32, asked, wanted, send, recv, halo_send, halo_recv, parts, part_energy, halo_spec,
    spec, rs, temps, x0, x1, done,
    ask_send_sem, ask_recv_sem, send_sem, recv_sem, halo_send_sem, halo_recv_sem, local_sem, done_sem, spec_sem, rs_sem,
):
    me = lax.axis_index("tmpl")
    z = lax.axis_index("sta")
    above = lax.rem(z + 1, depth)
    below = lax.rem(z + depth - 1, depth)

    y, x, core = me // 8, lax.rem(me // 2, 4), lax.rem(me, 2)

    def place(up, right, other):
        return lax.rem(y + up + 8, 4) * 8 + lax.rem(x + right + 8, 4) * 2 + lax.rem(core + other, 2)

    def steps(i):
        return lax.rem(i // 4, 4), lax.rem(i, 4), i // 16

    def ahead(i):
        up, right, other = steps(i)
        return place(up, right, other)

    def behind(i):
        up, right, other = steps(i)
        return place(-up, -right, other)

    barrier = pltpu.get_barrier_semaphore()

    def greet(i, carry):
        pl.semaphore_signal(barrier, inc=1, device_id={"tmpl": ahead(i)}, device_id_type=MESH)
        return carry

    lax.fori_loop(1, count, greet, 0)
    pl.semaphore_signal(barrier, inc=1, device_id={"sta": above}, device_id_type=MESH)
    pl.semaphore_signal(barrier, inc=1, device_id={"sta": below}, device_id_type=MESH)

    def widen(i, carry):
        block = rec_ref[i].astype(jnp.float32)
        for g in range(4):
            rec32[g, pl.ds(pl.multiple_of(i * 32, 32), 32), :] = block[:, g * 128:(g + 1) * 128]
        return carry

    lax.fori_loop(0, 24, widen, 0)
    pl.semaphore_wait(barrier, count + 1)

    def ask_copy(i):
        return pltpu.make_async_remote_copy(
            src_ref=ask_ref.at[ahead(i)], dst_ref=asked.at[i],
            send_sem=ask_send_sem.at[i], recv_sem=ask_recv_sem.at[i],
            device_id={"tmpl": ahead(i)}, device_id_type=MESH,
        )

    def ask_start(i, carry):
        ask_copy(i).start()
        return carry

    lax.fori_loop(1, count, ask_start, 0)
    asked[0] = ask_ref[me]

    lane = lax.broadcasted_iota(jnp.int32, (128, 128), 1)

    def template_block(n, carry):
        first = pl.multiple_of(n * 128, 128)
        pieces = [tmp_ref[c, pl.ds(first, 128), :] for c in range(3)]
        energy = sum(jnp.sum(jnp.square(p.astype(jnp.float32)), axis=1, keepdims=True) for p in pieces)
        factor = lax.rsqrt(energy / SCALE + EPSILON) / SCALE
        for c in range(3):
            found = mm(pieces[c], fwd_ref[...]) * factor
            for g in range(4):
                base = n * 4096 + g * 8
                temps[pl.ds(base + c, 128, stride=32), :] = found[:, g * 128:(g + 1) * 128]
                temps[pl.ds(base + c + 3, 128, stride=32), :] = found[:, TL + g * 128:TL + (g + 1) * 128]
        for g in range(4):
            for row in (6, 7):
                temps[pl.ds(n * 4096 + g * 8 + row, 128, stride=32), :] = jnp.zeros((128, 128), jnp.float32)
        return carry

    def ask_wait(i, carry):
        ask_copy(i).wait()
        return carry

    lax.fori_loop(1, count, ask_wait, 0)
    to_scalar = pltpu.make_async_copy(asked, wanted, local_sem.at[0])
    to_scalar.start()
    to_scalar.wait()

    def gather(i):
        rows = []
        for f in range(FETCH):
            s = wanted[i, 0, f]
            for c in range(3):
                rows.append(
                    jnp.concatenate(
                        [rec32[g, pl.ds(c * 32 + s, 8, stride=96), :] for g in range(4)], axis=1
                    )
                )
        return jnp.concatenate(rows, axis=0).astype(jnp.bfloat16)

    def data_copy(i):
        return pltpu.make_async_remote_copy(
            src_ref=send.at[i], dst_ref=recv.at[i],
            send_sem=send_sem.at[i], recv_sem=recv_sem.at[i],
            device_id={"tmpl": behind(i)}, device_id_type=MESH,
        )

    def data_start(i, carry):
        send[i] = gather(i)
        data_copy(i).start()
        return carry

    lax.fori_loop(1, count, data_start, 0)
    recv[0] = gather(0)

    lax.fori_loop(0, 4, template_block, 0)
    out_t = pltpu.make_async_copy(temps, t_out, local_sem.at[1])
    out_t.start()

    x1[...] = jnp.zeros_like(x1)
    lane8 = lax.broadcasted_iota(jnp.int32, (8, 128), 1)

    def pair_at(place):
        return jnp.maximum(order_s[0, jnp.maximum(place, 0)], 0)

    def cross_block(block, x):
        for i in range(0, PB, 2):
            templates, stations = [], []
            for k in range(2):
                q = pair_at(block * PB + i + k)
                base = slot_s[q] * 3
                templates.append(
                    lambda g, q=q: temps[pl.ds(q * 32 + g * 8, 8), :]
                )
                stations.append(lambda g, c, base=base: spec[base + c, :, pl.ds(g * 128, 128)])
            two_pairs(lane8, x, i, templates, stations)

    def invert_block(block, x):
        lagged = mm(x[...], inv_ref[...])
        for i in range(PB):
            place = block * PB + i
            done[place + PB] = lagged[i * 8:i * 8 + 8] * rs[slot_s[pair_at(place)]]

    def done_copy(n):
        rows = pl.ds(n * 32, 32)
        return pltpu.make_async_copy(done.at[rows], done_out.at[rows], done_sem.at[n])

    def pair_turn(n, carry):
        invert_block(2 * n - 1, x1)
        cross_block(2 * n, x0)
        invert_block(2 * n, x0)
        cross_block(2 * n + 1, x1)
        done_copy(n).start()
        return carry

    def stage(k):
        lax.fori_loop(jnp.maximum(2 * k - 1, 0), 2 * k + 1, pair_turn, 0)

    row = lax.broadcasted_iota(jnp.int32, (48, PER * ROWS), 0)
    col = lax.broadcasted_iota(jnp.int32, (48, PER * ROWS), 1)
    pick = (col == (row % 16) * 24 + (row // 16) * 8).astype(jnp.bfloat16)
    sample = lax.broadcasted_iota(jnp.int32, (TL, TL), 0)
    lag = lax.broadcasted_iota(jnp.int32, (TL, TL), 1)
    later = (sample >= lag).astype(jnp.bfloat16)
    earlier = (sample < lag).astype(jnp.bfloat16)
    last = lax.broadcasted_iota(jnp.int32, (8, 128), 0) == 7
    odd = jnp.where(lax.broadcasted_iota(jnp.int32, (8, 128), 1) % 2 == 0, 1.0, -1.0)

    def halo_copy(g):
        return pltpu.make_async_remote_copy(
            src_ref=halo_send.at[g], dst_ref=halo_recv.at[g],
            send_sem=halo_send_sem.at[g], recv_sem=halo_recv_sem.at[g],
            device_id={"sta": below}, device_id_type=MESH,
        )

    def main_part(g, slot):
        for k in range(PER):
            i = g * PER + k

            @pl.when(i > 0)
            def _():
                data_copy(i).wait_recv()

        block = recv[pl.ds(g * PER, PER)].reshape(PER * ROWS, TL)
        halo_send[g] = mm(pick, block).astype(jnp.bfloat16)
        halo_copy(g).start()
        for n in range(4):
            columns = pl.ds(n * 256, 256)
            parts[slot, :, columns] = mm(block, fwd_ref[:, columns])
        squares = jnp.square(block.astype(jnp.float32)).reshape(16, 3, 8, TL)
        squares = (squares[:, 0] + squares[:, 1] + squares[:, 2]).reshape(128, TL)
        high, low = split(squares)
        part_energy[slot, 0] = mm(high, later) + mm(low, later)
        part_energy[slot, 1] = mm(high, earlier) + mm(low, earlier)

    def station_at(g, s):
        return ahead(g * PER + s // FETCH) * FETCH + lax.rem(s, FETCH)

    def halo_part(g, slot):
        halo_copy(g).wait_recv()
        block = jnp.where(z == depth - 1, jnp.zeros((48, TL), jnp.bfloat16), halo_recv[g])
        found = mm(block, fwd_ref[...])
        for n in range(8):
            halo_spec[n, 0:48, :] = found[:, n * 128:(n + 1) * 128]
        squares = jnp.square(block.astype(jnp.float32))
        high, low = split(squares[0:16] + squares[16:32] + squares[32:48])
        energy = mm(high, earlier) + mm(low, earlier)
        for n in range(4):
            halo_spec[n, 48:64, :] = energy[:, n * 128:(n + 1) * 128]

        def station(s, carry):
            for c in range(3):
                base = pl.multiple_of(s * 24 + c * 8, 8)
                halves = []
                for n in range(8):
                    now = parts[slot, pl.ds(base, 8), pl.ds(n * 128, 128)]
                    beyond = halo_spec[n, pl.ds(c * 16 + s, 8, stride=0), :]
                    following = jnp.where(last, beyond, pltpu.roll(now, 7, 0))
                    halves.append(now + odd * following)
                real = jnp.concatenate(halves[:4], axis=1)
                imag = jnp.concatenate(halves[4:], axis=1)
                spec[station_at(g, s) * 3 + c] = jnp.concatenate([real, imag], axis=0).astype(jnp.bfloat16)
            base = pl.multiple_of(s * 8, 8)
            for n in range(4):
                columns = pl.ds(n * 128, 128)
                early = part_energy[slot, 1, pl.ds(base, 8), columns]
                beyond = halo_spec[n, pl.ds(48 + s, 8, stride=0), :]
                early = jnp.where(last, beyond, pltpu.roll(early, 7, 0))
                total = part_energy[slot, 0, pl.ds(base, 8), columns] + early
                rs[station_at(g, s), :, columns] = lax.rsqrt(total / SCALE + EPSILON)
            return carry

        lax.fori_loop(0, 16, station, 0)

        def leave(k, carry):
            spec_copy(g * PER + k).start()
            rs_copy(g * PER + k).start()
            return carry

        lax.fori_loop(0, PER, leave, 0)

    def spec_copy(i):
        rows = pl.ds(ahead(i) * (FETCH * 3), FETCH * 3)
        return pltpu.make_async_copy(spec.at[rows], spec_out.at[rows], spec_sem.at[i])

    def rs_copy(i):
        rows = pl.ds(ahead(i) * FETCH, FETCH)
        return pltpu.make_async_copy(rs.at[rows], rs_out.at[rows], rs_sem.at[i])

    main_part(0, 0)

    def turn(g, carry):
        main_part(g, lax.rem(g, 2))
        halo_part(g - 1, lax.rem(g - 1, 2))
        stage(g - 1)
        return carry

    lax.fori_loop(1, GROUPS, turn, 0)
    halo_part(GROUPS - 1, (GROUPS - 1) % 2)
    lax.fori_loop(2 * GROUPS - 3, PAIRS // 32, pair_turn, 0)
    invert_block(PAIRS // PB - 1, x1)
    rest = pltpu.make_async_copy(done.at[pl.ds(PAIRS, PB)], done_out.at[pl.ds(PAIRS, PB)], local_sem.at[3])
    rest.start()

    def finish(i, carry):
        data_copy(i).wait_send()
        return carry

    lax.fori_loop(1, count, finish, 0)

    def finish_group(g, carry):
        halo_copy(g).wait_send()
        return carry

    def finish_source(i, carry):
        spec_copy(i).wait()
        rs_copy(i).wait()
        return carry

    def finish_places(n, carry):
        done_copy(n).wait()
        return carry

    lax.fori_loop(0, GROUPS, finish_group, 0)
    lax.fori_loop(0, count, finish_source, 0)
    lax.fori_loop(0, PAIRS // 32, finish_places, 0)
    rest.wait()
    out_t.wait()


def exchange_call(mesh, order, slot, rec, ask, templates, forward, inverse):
    count, depth = mesh.shape["tmpl"], mesh.shape["sta"]
    vmem = pl.BlockSpec(memory_space=pltpu.VMEM)
    hbm = pl.BlockSpec(memory_space=pl.ANY)
    smem = pl.BlockSpec(memory_space=pltpu.SMEM)
    f32, bf16 = jnp.float32, jnp.bfloat16
    slots = count * FETCH
    return pl.pallas_call(
        functools.partial(exchange_kernel, count, depth),
        out_shape=[
            jax.ShapeDtypeStruct((slots * 3, 16, TL), bf16),
            jax.ShapeDtypeStruct((slots, 8, TL), f32),
            jax.ShapeDtypeStruct((512 * 32, 128), f32),
            jax.ShapeDtypeStruct((PAIRS + PB, 8, TL), f32),
        ],
        in_specs=[smem] * 2 + [vmem] * 5,
        out_specs=[hbm] * 4,
        scratch_shapes=[
            pltpu.VMEM((4, 768, 128), f32),
            pltpu.VMEM((count, 1, 128), jnp.int32),
            pltpu.SMEM((count, 1, 128), jnp.int32),
            pltpu.VMEM((count, ROWS, TL), bf16),
            pltpu.VMEM((count, ROWS, TL), bf16),
            pltpu.VMEM((GROUPS, 48, TL), bf16),
            pltpu.VMEM((GROUPS, 48, TL), bf16),
            pltpu.VMEM((2, PER * ROWS, NBINS), f32),
            pltpu.VMEM((2, 2, 128, TL), f32),
            pltpu.VMEM((8, 64, 128), f32),
            pltpu.VMEM((slots * 3, 16, TL), bf16),
            pltpu.VMEM((slots, 8, TL), f32),
            pltpu.VMEM((512 * 32, 128), f32),
            pltpu.VMEM((PB * 8, NBINS), bf16),
            pltpu.VMEM((PB * 8, NBINS), bf16),
            pltpu.VMEM((PAIRS + PB, 8, TL), f32),
            pltpu.SemaphoreType.DMA((count,)),
            pltpu.SemaphoreType.DMA((count,)),
            pltpu.SemaphoreType.DMA((count,)),
            pltpu.SemaphoreType.DMA((count,)),
            pltpu.SemaphoreType.DMA((GROUPS,)),
            pltpu.SemaphoreType.DMA((GROUPS,)),
            pltpu.SemaphoreType.DMA((4,)),
            pltpu.SemaphoreType.DMA((PAIRS // 32,)),
            pltpu.SemaphoreType.DMA((count,)),
            pltpu.SemaphoreType.DMA((count,)),
        ],
        compiler_params=pltpu.CompilerParams(
            collective_id=0, has_side_effects=True, vmem_limit_bytes=60 * 2**20
        ),
        name="exchange",
    )(order, slot, rec, ask, templates, forward, inverse)


CHUNKS = 8


def pair_kernel(
    order_ref, slot_ref, tmpl_ref, off_ref, live_ref, inv_ref, pt_ref, spec_in, rs_in, t_in, done_in,
    out_ref, head_ref,
    acc, done, x, y, spec, rs, temps, done_sem, spec_sem, rs_sem, t_sem,
):
    live = live_ref[0]
    lane = lax.broadcasted_iota(jnp.int32, (8, 128), 1)

    def chunk(n):
        rows = pl.ds(n * (PAIRS // CHUNKS), PAIRS // CHUNKS)
        return pltpu.make_async_copy(
            done_in.at[pl.ds(n * (PAIRS // CHUNKS) + PB, PAIRS // CHUNKS)], done.at[rows], done_sem.at[n]
        )

    for n in range(CHUNKS):
        chunk(n).start()
    acc[...] = jnp.zeros_like(acc)

    def add(place, row):
        q = order_ref[0, place]
        j = jnp.where(q >= 0, tmpl_ref[jnp.maximum(q, 0)], T_DEV)
        o = off_ref[jnp.maximum(q, 0)]
        coarse = lax.shift_right_logical(o, 7)
        fine = o & 127
        low = lane < 128 - fine
        turned = [pltpu.roll(row[:, g * 128:(g + 1) * 128], 128 - fine, 1) for g in range(4)]
        parts = [jnp.where(low, 0.0, turned[0])]
        for g in range(3):
            parts.append(jnp.where(low, turned[g], turned[g + 1]))
        parts.append(jnp.where(low, turned[3], 0.0))
        base = pl.multiple_of(j * 64 + 24 - 8 * coarse, 8)
        acc[pl.ds(base, 40), :] += jnp.concatenate(parts, axis=0)

    def add_some(b, carry):
        for i in range(8):
            add(b * 8 + i, done[b * 8 + i])
        return carry

    for n in range(CHUNKS):
        chunk(n).wait()
        lax.fori_loop(n * (PAIRS // CHUNKS // 8), (n + 1) * (PAIRS // CHUNKS // 8), add_some, 0)

    def copies(q, i):
        s = slot_ref[q]
        return (
            pltpu.make_async_copy(spec_in.at[pl.ds(s * 3, 3)], spec.at[i], spec_sem.at[i]),
            pltpu.make_async_copy(rs_in.at[s], rs.at[i], rs_sem.at[i]),
            pltpu.make_async_copy(t_in.at[pl.ds(pl.multiple_of(q * 32, 32), 32)], temps.at[i], t_sem.at[i]),
        )

    def late_block(first):
        qs = [jnp.maximum(order_ref[0, first + i], 0) for i in range(PB)]
        for i, q in enumerate(qs):
            for copy in copies(q, i):
                copy.start()
        for i, q in enumerate(qs):
            for copy in copies(q, i):
                copy.wait()
        for i in range(0, PB, 2):
            two_pairs(
                lane, x, i,
                [lambda g, k=k: temps[k, pl.ds(g * 8, 8), :] for k in (i, i + 1)],
                [lambda g, c, k=k: spec[k, c, :, pl.ds(g * 128, 128)] for k in (i, i + 1)],
            )
        y[...] = mm(x[...], inv_ref[...])
        for i in range(PB):
            add(first + i, y[pl.ds(i * 8, 8), :] * rs[i])

    def late(n, carry):
        first = PAIRS + n * PB

        @pl.when(order_ref[0, first] >= 0)
        def _():
            late_block(first)

        return carry

    @pl.when(order_ref[0, PAIRS] >= 0)
    def _():
        lax.fori_loop(0, (PLACES - PAIRS) // PB, late, 0)

    same = (pt_ref[...] == lax.broadcasted_iota(jnp.int32, (T_DEV, PAIRS), 0)) & (
        lax.broadcasted_iota(jnp.int32, (T_DEV, PAIRS), 1) < live
    )
    counts = jnp.sum(same.astype(jnp.float32), axis=1, keepdims=True)
    scale = jnp.sqrt(SCALE / counts)
    for g in range(4):
        lanes = pl.ds(g * 128, 128)
        head_ref[:, lanes] = acc[pl.ds(g * 8, T_DEV, stride=64), :] * scale
        for h in range(8):
            v = acc[pl.ds(32 + g * 8 + h, T_DEV, stride=64), :]
            if h < 7:
                v = v + acc[pl.ds(g * 8 + h + 1, T_DEV, stride=64), :]
            out_ref[h, :, lanes] = v * scale


def pair_call(order, slot, tmpl, off, live, inverse, spec, rs, t, done):
    smem = pl.BlockSpec(memory_space=pltpu.SMEM)
    vmem = pl.BlockSpec(memory_space=pltpu.VMEM)
    hbm = pl.BlockSpec(memory_space=pl.ANY)
    f32, bf16 = jnp.float32, jnp.bfloat16
    return pl.pallas_call(
        pair_kernel,
        out_shape=[jax.ShapeDtypeStruct((8, T_DEV, TL), f32), jax.ShapeDtypeStruct((T_DEV, TL), f32)],
        in_specs=[smem] * 5 + [vmem] * 2 + [hbm] * 4,
        out_specs=[vmem] * 2,
        scratch_shapes=[
            pltpu.VMEM(((T_DEV + 1) * 64, 128), f32),
            pltpu.VMEM((PAIRS, 8, TL), f32),
            pltpu.VMEM((PB * 8, NBINS), bf16),
            pltpu.VMEM((PB * 8, TL), f32),
            pltpu.VMEM((PB, 3, 16, TL), bf16),
            pltpu.VMEM((PB, 8, TL), f32),
            pltpu.VMEM((PB, 32, 128), f32),
            pltpu.SemaphoreType.DMA((CHUNKS,)),
            pltpu.SemaphoreType.DMA((PB,)),
            pltpu.SemaphoreType.DMA((PB,)),
            pltpu.SemaphoreType.DMA((PB,)),
        ],
        compiler_params=pltpu.CompilerParams(vmem_limit_bytes=40 * 2**20),
        name="pairs",
    )(order, slot, tmpl, off, live, inverse, tmpl.reshape(1, PAIRS), spec, rs, t, done)


def shards(mesh, records, templates, requests, pair_slot, pair_template, pair_offset, live_pairs):
    count, depth = mesh.shape["tmpl"], mesh.shape["sta"]
    rec = jnp.transpose(records, (0, 2, 1, 3)).reshape(24, 32, TL)
    ask = jnp.pad(requests.reshape(count, 1, FETCH), ((0, 0), (0, 0), (0, 128 - FETCH)))
    order = place_call(pair_slot, live_pairs)
    spec, rs, temps, done = exchange_call(
        mesh, order, pair_slot, rec, ask, jnp.transpose(templates, (1, 0, 2)), jnp.asarray(FORWARD),
        jnp.asarray(INVERSE),
    )
    out, head = pair_call(
        order, pair_slot, pair_template, pair_offset, live_pairs, jnp.asarray(INVERSE), spec, rs, temps, done
    )
    head = lax.ppermute(head, "sta", [(i, i - 1) for i in range(1, depth)])
    return out.at[7].add(head)


def solution(mesh):
    in_specs = (
        P("sta", "tmpl", None, None),
        P("tmpl", None, None),
        P("tmpl", None, None),
        P("tmpl"),
        P("tmpl"),
        P("tmpl"),
        P("tmpl"),
    )
    return jax.shard_map(
        functools.partial(shards, mesh), mesh=mesh, in_specs=in_specs,
        out_specs=P("sta", "tmpl", None), check_vma=False,
    )
```

```python
import functools

import jax
import jax.numpy as jnp
import numpy as np
from jax import lax
from jax.experimental import pallas as pl
from jax.experimental.pallas import tpu as pltpu
from jax.sharding import PartitionSpec as P

TL = 512
NBINS = 2 * TL
T_DEV = 32
FETCH = 4
SCALE = 3.0 * TL
EPSILON = 1e-05
MESH = pl.DeviceIdType.MESH
PB = 16
PAIRS = 512
PLACES = 1024


def dft_tables():
    n = np.arange(TL)[:, None]
    k = np.arange(TL)[None, :]
    angles = (n * k % NBINS) * (2.0 * np.pi / NBINS)
    parity = np.where(n % 2 == 0, 1.0, -1.0)
    second = np.where(k == 0, parity, -np.sin(angles))
    forward = np.concatenate([np.cos(angles), second], axis=1).astype(jnp.bfloat16)
    alternate = np.where(k % 2 == 0, 1.0, -1.0)
    cosine_rows = np.where(n == 0, 1.0, 2.0 * np.cos(angles)) / NBINS
    sine_rows = np.where(n == 0, alternate, -2.0 * np.sin(angles)) / NBINS
    inverse = np.concatenate([cosine_rows, sine_rows], axis=0).astype(jnp.bfloat16)
    return forward, inverse


FORWARD, INVERSE = dft_tables()

GROUPS = 8
PER = 4
ROWS = FETCH * 24


def split(value):
    high = value.astype(jnp.bfloat16)
    low = (value - high.astype(jnp.float32)).astype(jnp.bfloat16)
    return high, low


def mm(left, right):
    return jnp.dot(left, right, preferred_element_type=jnp.float32)


def cross_terms(lane, group, template, station):
    real = imag = None
    for c in range(3):
        rows = station(c).astype(jnp.float32)
        br, bm = rows[:8], rows[8:]
        ar = jnp.broadcast_to(template[c:c + 1], (8, 128))
        am = jnp.broadcast_to(template[c + 3:c + 4], (8, 128))
        cr = ar
        if group == 0:
            cr = jnp.where(lane == 0, am, ar)
            am = jnp.where(lane == 0, 0.0, am)
        r = ar * br + am * bm
        m = cr * bm - am * br
        real = r if real is None else real + r
        imag = m if imag is None else imag + m
    return real, imag


def two_pairs(lane, x, i, templates, stations):
    for g in range(4):
        terms = [cross_terms(lane, g, t(g), functools.partial(s, g)) for t, s in zip(templates, stations)]
        for half in range(2):
            rows = jnp.concatenate([t[half] for t in terms], axis=0).astype(jnp.bfloat16)
            x[pl.ds(i * 8, 16), pl.ds(half * TL + g * 128, 128)] = rows


def exchange_kernel(
    count, depth, slot_s, rec_ref, ask_ref, tmp_ref, fwd_ref, inv_ref, slot_ref, live_s,
    spec_out, rs_out, t_out, done_out, order_out,
    rec32, asks, asked, wanted, send, recv, halo_send, halo_recv, parts, part_energy, halo_spec,
    spec, rs, temps, order, order_s, x0, x1, done,
    ask_send_sem, ask_recv_sem, send_sem, recv_sem, halo_send_sem, halo_recv_sem, local_sem, done_sem, spec_sem, rs_sem,
):
    me = lax.axis_index("tmpl")
    z = lax.axis_index("sta")
    above = lax.rem(z + 1, depth)
    below = lax.rem(z + depth - 1, depth)

    y, x, core = me // 8, lax.rem(me // 2, 4), lax.rem(me, 2)

    def place(up, right, other):
        return lax.rem(y + up + 8, 4) * 8 + lax.rem(x + right + 8, 4) * 2 + lax.rem(core + other, 2)

    def steps(i):
        return lax.rem(i // 4, 4), lax.rem(i, 4), i // 16

    def ahead(i):
        up, right, other = steps(i)
        return place(up, right, other)

    def behind(i):
        up, right, other = steps(i)
        return place(-up, -right, other)

    barrier = pltpu.get_barrier_semaphore()

    def greet(i, carry):
        pl.semaphore_signal(barrier, inc=1, device_id={"tmpl": ahead(i)}, device_id_type=MESH)
        return carry

    lax.fori_loop(1, count, greet, 0)
    pl.semaphore_signal(barrier, inc=1, device_id={"sta": above}, device_id_type=MESH)
    pl.semaphore_signal(barrier, inc=1, device_id={"sta": below}, device_id_type=MESH)

    def widen(i, carry):
        block = rec_ref[i].astype(jnp.float32)
        for g in range(4):
            rec32[g, pl.ds(pl.multiple_of(i * 32, 32), 32), :] = block[:, g * 128:(g + 1) * 128]
        return carry

    lax.fori_loop(0, 24, widen, 0)
    rows = lax.broadcasted_iota(jnp.int32, (count, count), 0)
    lanes = lax.broadcasted_iota(jnp.int32, (count, count), 1)
    table = jnp.zeros((count, 128), jnp.int32)
    for f in range(FETCH):
        column = jnp.sum(jnp.where(rows == lanes, ask_ref[f:f + 1, :], 0), axis=1, keepdims=True)
        table = jnp.where(lax.broadcasted_iota(jnp.int32, (count, 128), 1) == f, column, table)
    for d in range(count):
        asks[d] = table[d:d + 1, :]
    pl.semaphore_wait(barrier, count + 1)

    def ask_copy(i):
        return pltpu.make_async_remote_copy(
            src_ref=asks.at[ahead(i)], dst_ref=asked.at[i],
            send_sem=ask_send_sem.at[i], recv_sem=ask_recv_sem.at[i],
            device_id={"tmpl": ahead(i)}, device_id_type=MESH,
        )

    def ask_start(i, carry):
        ask_copy(i).start()
        return carry

    lax.fori_loop(1, count, ask_start, 0)
    asked[0] = asks[me]

    lane = lax.broadcasted_iota(jnp.int32, (128, 128), 1)

    def template_block(n, carry):
        first = pl.multiple_of(n * 128, 128)
        pieces = [tmp_ref[c, pl.ds(first, 128), :] for c in range(3)]
        energy = sum(jnp.sum(jnp.square(p.astype(jnp.float32)), axis=1, keepdims=True) for p in pieces)
        factor = lax.rsqrt(energy / SCALE + EPSILON) / SCALE
        for c in range(3):
            found = mm(pieces[c], fwd_ref[...]) * factor
            for g in range(4):
                base = n * 4096 + g * 8
                temps[pl.ds(base + c, 128, stride=32), :] = found[:, g * 128:(g + 1) * 128]
                temps[pl.ds(base + c + 3, 128, stride=32), :] = found[:, TL + g * 128:TL + (g + 1) * 128]
        for g in range(4):
            for row in (6, 7):
                temps[pl.ds(n * 4096 + g * 8 + row, 128, stride=32), :] = jnp.zeros((128, 128), jnp.float32)
        return carry

    def ask_wait(i, carry):
        ask_copy(i).wait()
        return carry

    lax.fori_loop(1, count, ask_wait, 0)
    to_scalar = pltpu.make_async_copy(asked, wanted, local_sem.at[0])
    to_scalar.start()
    to_scalar.wait()

    def gather(i):
        rows = []
        for f in range(FETCH):
            s = wanted[i, 0, f]
            for c in range(3):
                rows.append(
                    jnp.concatenate(
                        [rec32[g, pl.ds(c * 32 + s, 8, stride=96), :] for g in range(4)], axis=1
                    )
                )
        return jnp.concatenate(rows, axis=0).astype(jnp.bfloat16)

    def data_copy(i):
        return pltpu.make_async_remote_copy(
            src_ref=send.at[i], dst_ref=recv.at[i],
            send_sem=send_sem.at[i], recv_sem=recv_sem.at[i],
            device_id={"tmpl": behind(i)}, device_id_type=MESH,
        )

    def data_start(i, carry):
        send[i] = gather(i)
        data_copy(i).start()
        return carry

    lax.fori_loop(1, count, data_start, 0)
    recv[0] = gather(0)

    lax.fori_loop(0, 4, template_block, 0)
    out_t = pltpu.make_async_copy(temps, t_out, local_sem.at[1])
    out_t.start()

    f32, bf16 = jnp.float32, jnp.bfloat16
    i32 = jnp.int32
    live = live_s[0]
    pair_row = lax.broadcasted_iota(i32, (PAIRS, PAIRS), 1)
    pair_col = lax.broadcasted_iota(i32, (PAIRS, PAIRS), 0)
    source = lax.shift_right_logical(slot_ref[...], 2)
    key_row = ((source + me) & 1) * 4 + ((lax.shift_right_logical(source, 3) - y) & 3)
    key_row = jnp.where(pair_row[:1] < live, key_row, GROUPS)
    key_col = jnp.sum(jnp.where(pair_row == pair_col, key_row, 0), axis=1, keepdims=True)
    ahead_of = (key_row < key_col) | ((key_row == key_col) & (pair_row < pair_col))
    rank_col = jnp.sum(ahead_of.astype(i32), axis=1, keepdims=True)
    group_row = lax.broadcasted_iota(i32, (PAIRS, 128), 1)
    below_count = jnp.sum((key_col < group_row).astype(i32), axis=0, keepdims=True)
    gap = jnp.maximum(64 * group_row[:1] - 32, 0) - below_count
    gap = jnp.where((group_row <= key_col) & (group_row < GROUPS), gap, 0)
    place_col = rank_col + jnp.max(gap, axis=1, keepdims=True)
    place_col = jnp.where(key_col < GROUPS, place_col, 2 * PLACES)
    for n in range(PLACES // 128):
        here = place_col == group_row + n * 128
        found = jnp.sum(jnp.where(here, pair_col[:, :128] + 1, 0), axis=0, keepdims=True)
        order[:, pl.ds(n * 128, 128)] = found - 1
    order_copies = (
        pltpu.make_async_copy(order, order_s, local_sem.at[0]),
        pltpu.make_async_copy(order, order_out, local_sem.at[2]),
    )
    for copy in order_copies:
        copy.start()
    for copy in order_copies:
        copy.wait()
    x1[...] = jnp.zeros_like(x1)
    lane8 = lax.broadcasted_iota(jnp.int32, (8, 128), 1)

    def pair_at(place):
        return jnp.maximum(order_s[0, jnp.maximum(place, 0)], 0)

    def cross_block(block, x):
        for i in range(0, PB, 2):
            templates, stations = [], []
            for k in range(2):
                q = pair_at(block * PB + i + k)
                base = slot_s[q] * 3
                templates.append(
                    lambda g, q=q: temps[pl.ds(q * 32 + g * 8, 8), :]
                )
                stations.append(lambda g, c, base=base: spec[base + c, :, pl.ds(g * 128, 128)])
            two_pairs(lane8, x, i, templates, stations)

    def invert_block(block, x):
        lagged = mm(x[...], inv_ref[...])
        for i in range(PB):
            place = block * PB + i
            done[place + PB] = lagged[i * 8:i * 8 + 8] * rs[slot_s[pair_at(place)]]

    def done_copy(n):
        rows = pl.ds(n * 32, 32)
        return pltpu.make_async_copy(done.at[rows], done_out.at[rows], done_sem.at[n])

    def pair_turn(n, carry):
        invert_block(2 * n - 1, x1)
        cross_block(2 * n, x0)
        invert_block(2 * n, x0)
        cross_block(2 * n + 1, x1)
        done_copy(n).start()
        return carry

    def stage(k):
        lax.fori_loop(jnp.maximum(2 * k - 1, 0), 2 * k + 1, pair_turn, 0)

    row = lax.broadcasted_iota(jnp.int32, (48, PER * ROWS), 0)
    col = lax.broadcasted_iota(jnp.int32, (48, PER * ROWS), 1)
    pick = (col == (row % 16) * 24 + (row // 16) * 8).astype(jnp.bfloat16)
    sample = lax.broadcasted_iota(jnp.int32, (TL, TL), 0)
    lag = lax.broadcasted_iota(jnp.int32, (TL, TL), 1)
    later = (sample >= lag).astype(jnp.bfloat16)
    earlier = (sample < lag).astype(jnp.bfloat16)
    last = lax.broadcasted_iota(jnp.int32, (8, 128), 0) == 7
    odd = jnp.where(lax.broadcasted_iota(jnp.int32, (8, 128), 1) % 2 == 0, 1.0, -1.0)

    def halo_copy(g):
        return pltpu.make_async_remote_copy(
            src_ref=halo_send.at[g], dst_ref=halo_recv.at[g],
            send_sem=halo_send_sem.at[g], recv_sem=halo_recv_sem.at[g],
            device_id={"sta": below}, device_id_type=MESH,
        )

    def main_part(g, slot):
        for k in range(PER):
            i = g * PER + k

            @pl.when(i > 0)
            def _():
                data_copy(i).wait_recv()

        block = recv[pl.ds(g * PER, PER)].reshape(PER * ROWS, TL)
        halo_send[g] = mm(pick, block).astype(jnp.bfloat16)
        halo_copy(g).start()
        for n in range(4):
            columns = pl.ds(n * 256, 256)
            parts[slot, :, columns] = mm(block, fwd_ref[:, columns])
        squares = jnp.square(block.astype(jnp.float32)).reshape(16, 3, 8, TL)
        squares = (squares[:, 0] + squares[:, 1] + squares[:, 2]).reshape(128, TL)
        high, low = split(squares)
        part_energy[slot, 0] = mm(high, later) + mm(low, later)
        part_energy[slot, 1] = mm(high, earlier) + mm(low, earlier)

    def station_at(g, s):
        return ahead(g * PER + s // FETCH) * FETCH + lax.rem(s, FETCH)

    def halo_part(g, slot):
        halo_copy(g).wait_recv()
        block = jnp.where(z == depth - 1, jnp.zeros((48, TL), jnp.bfloat16), halo_recv[g])
        found = mm(block, fwd_ref[...])
        for n in range(8):
            halo_spec[n, 0:48, :] = found[:, n * 128:(n + 1) * 128]
        squares = jnp.square(block.astype(jnp.float32))
        high, low = split(squares[0:16] + squares[16:32] + squares[32:48])
        energy = mm(high, earlier) + mm(low, earlier)
        for n in range(4):
            halo_spec[n, 48:64, :] = energy[:, n * 128:(n + 1) * 128]

        def station(s, carry):
            for c in range(3):
                base = pl.multiple_of(s * 24 + c * 8, 8)
                halves = []
                for n in range(8):
                    now = parts[slot, pl.ds(base, 8), pl.ds(n * 128, 128)]
                    beyond = halo_spec[n, pl.ds(c * 16 + s, 8, stride=0), :]
                    following = jnp.where(last, beyond, pltpu.roll(now, 7, 0))
                    halves.append(now + odd * following)
                real = jnp.concatenate(halves[:4], axis=1)
                imag = jnp.concatenate(halves[4:], axis=1)
                spec[station_at(g, s) * 3 + c] = jnp.concatenate([real, imag], axis=0).astype(jnp.bfloat16)
            base = pl.multiple_of(s * 8, 8)
            for n in range(4):
                columns = pl.ds(n * 128, 128)
                early = part_energy[slot, 1, pl.ds(base, 8), columns]
                beyond = halo_spec[n, pl.ds(48 + s, 8, stride=0), :]
                early = jnp.where(last, beyond, pltpu.roll(early, 7, 0))
                total = part_energy[slot, 0, pl.ds(base, 8), columns] + early
                rs[station_at(g, s), :, columns] = lax.rsqrt(total / SCALE + EPSILON)
            return carry

        lax.fori_loop(0, 16, station, 0)

        def leave(k, carry):
            spec_copy(g * PER + k).start()
            rs_copy(g * PER + k).start()
            return carry

        lax.fori_loop(0, PER, leave, 0)

    def spec_copy(i):
        rows = pl.ds(ahead(i) * (FETCH * 3), FETCH * 3)
        return pltpu.make_async_copy(spec.at[rows], spec_out.at[rows], spec_sem.at[i])

    def rs_copy(i):
        rows = pl.ds(ahead(i) * FETCH, FETCH)
        return pltpu.make_async_copy(rs.at[rows], rs_out.at[rows], rs_sem.at[i])

    main_part(0, 0)

    def turn(g, carry):
        main_part(g, lax.rem(g, 2))
        halo_part(g - 1, lax.rem(g - 1, 2))
        stage(g - 1)
        return carry

    lax.fori_loop(1, GROUPS, turn, 0)
    halo_part(GROUPS - 1, (GROUPS - 1) % 2)
    lax.fori_loop(2 * GROUPS - 3, PAIRS // 32, pair_turn, 0)
    invert_block(PAIRS // PB - 1, x1)
    rest = pltpu.make_async_copy(done.at[pl.ds(PAIRS, PB)], done_out.at[pl.ds(PAIRS, PB)], local_sem.at[3])
    rest.start()

    def finish(i, carry):
        data_copy(i).wait_send()
        return carry

    lax.fori_loop(1, count, finish, 0)

    def finish_group(g, carry):
        halo_copy(g).wait_send()
        return carry

    def finish_source(i, carry):
        spec_copy(i).wait()
        rs_copy(i).wait()
        return carry

    def finish_places(n, carry):
        done_copy(n).wait()
        return carry

    lax.fori_loop(0, GROUPS, finish_group, 0)
    lax.fori_loop(0, count, finish_source, 0)
    lax.fori_loop(0, PAIRS // 32, finish_places, 0)
    rest.wait()
    out_t.wait()


def exchange_call(mesh, slot, rec, ask, templates, forward, inverse, live):
    count, depth = mesh.shape["tmpl"], mesh.shape["sta"]
    vmem = pl.BlockSpec(memory_space=pltpu.VMEM)
    hbm = pl.BlockSpec(memory_space=pl.ANY)
    smem = pl.BlockSpec(memory_space=pltpu.SMEM)
    f32, bf16 = jnp.float32, jnp.bfloat16
    slots = count * FETCH
    return pl.pallas_call(
        functools.partial(exchange_kernel, count, depth),
        out_shape=[
            jax.ShapeDtypeStruct((slots * 3, 16, TL), bf16),
            jax.ShapeDtypeStruct((slots, 8, TL), f32),
            jax.ShapeDtypeStruct((512 * 32, 128), f32),
            jax.ShapeDtypeStruct((PAIRS + PB, 8, TL), f32),
            jax.ShapeDtypeStruct((1, PLACES), jnp.int32),
        ],
        in_specs=[smem] + [vmem] * 6 + [smem],
        out_specs=[hbm] * 5,
        scratch_shapes=[
            pltpu.VMEM((4, 768, 128), f32),
            pltpu.VMEM((count, 1, 128), jnp.int32),
            pltpu.VMEM((count, 1, 128), jnp.int32),
            pltpu.SMEM((count, 1, 128), jnp.int32),
            pltpu.VMEM((count, ROWS, TL), bf16),
            pltpu.VMEM((count, ROWS, TL), bf16),
            pltpu.VMEM((GROUPS, 48, TL), bf16),
            pltpu.VMEM((GROUPS, 48, TL), bf16),
            pltpu.VMEM((2, PER * ROWS, NBINS), f32),
            pltpu.VMEM((2, 2, 128, TL), f32),
            pltpu.VMEM((8, 64, 128), f32),
            pltpu.VMEM((slots * 3, 16, TL), bf16),
            pltpu.VMEM((slots, 8, TL), f32),
            pltpu.VMEM((512 * 32, 128), f32),
            pltpu.VMEM((1, PLACES), jnp.int32),
            pltpu.SMEM((1, PLACES), jnp.int32),
            pltpu.VMEM((PB * 8, NBINS), bf16),
            pltpu.VMEM((PB * 8, NBINS), bf16),
            pltpu.VMEM((PAIRS + PB, 8, TL), f32),
            pltpu.SemaphoreType.DMA((count,)),
            pltpu.SemaphoreType.DMA((count,)),
            pltpu.SemaphoreType.DMA((count,)),
            pltpu.SemaphoreType.DMA((count,)),
            pltpu.SemaphoreType.DMA((GROUPS,)),
            pltpu.SemaphoreType.DMA((GROUPS,)),
            pltpu.SemaphoreType.DMA((4,)),
            pltpu.SemaphoreType.DMA((PAIRS // 32,)),
            pltpu.SemaphoreType.DMA((count,)),
            pltpu.SemaphoreType.DMA((count,)),
        ],
        compiler_params=pltpu.CompilerParams(
            collective_id=0, has_side_effects=True, vmem_limit_bytes=60 * 2**20
        ),
        name="exchange",
    )(slot, rec, ask, templates, forward, inverse, slot.reshape(1, PAIRS), live)


SUMS = 4
CHUNKS = 8


def pair_kernel(
    order_ref, slot_ref, tmpl_ref, off_ref, live_ref, inv_ref, pt_ref, spec_in, rs_in, t_in, done_in,
    out_ref, head_ref,
    sum0, sum1, sum2, sum3, done, x, y, spec, rs, temps, done_sem, spec_sem, rs_sem, t_sem,
):
    live = live_ref[0]
    lane = lax.broadcasted_iota(jnp.int32, (8, 128), 1)

    def chunk(n):
        rows = pl.ds(n * (PAIRS // CHUNKS), PAIRS // CHUNKS)
        return pltpu.make_async_copy(
            done_in.at[pl.ds(n * (PAIRS // CHUNKS) + PB, PAIRS // CHUNKS)], done.at[rows], done_sem.at[n]
        )

    for n in range(CHUNKS):
        chunk(n).start()
    sums = (sum0, sum1, sum2, sum3)
    for acc in sums:
        acc[...] = jnp.zeros_like(acc)

    def add(place, row, acc):
        q = order_ref[0, place]
        j = jnp.where(q >= 0, tmpl_ref[jnp.maximum(q, 0)], T_DEV)
        o = off_ref[jnp.maximum(q, 0)]
        coarse = lax.shift_right_logical(o, 7)
        fine = o & 127
        low = lane < 128 - fine
        turned = [pltpu.roll(row[:, g * 128:(g + 1) * 128], 128 - fine, 1) for g in range(4)]
        parts = [jnp.where(low, 0.0, turned[0])]
        for g in range(3):
            parts.append(jnp.where(low, turned[g], turned[g + 1]))
        parts.append(jnp.where(low, turned[3], 0.0))
        base = pl.multiple_of(j * 64 + 24 - 8 * coarse, 8)
        acc[pl.ds(base, 40), :] += jnp.concatenate(parts, axis=0)

    def add_some(b, carry):
        for i in range(8):
            add(b * 8 + i, done[b * 8 + i], sums[i % SUMS])
        return carry

    for n in range(CHUNKS):
        chunk(n).wait()
        lax.fori_loop(n * (PAIRS // CHUNKS // 8), (n + 1) * (PAIRS // CHUNKS // 8), add_some, 0)

    def copies(q, i):
        s = slot_ref[q]
        return (
            pltpu.make_async_copy(spec_in.at[pl.ds(s * 3, 3)], spec.at[i], spec_sem.at[i]),
            pltpu.make_async_copy(rs_in.at[s], rs.at[i], rs_sem.at[i]),
            pltpu.make_async_copy(t_in.at[pl.ds(pl.multiple_of(q * 32, 32), 32)], temps.at[i], t_sem.at[i]),
        )

    def late_block(first):
        qs = [jnp.maximum(order_ref[0, first + i], 0) for i in range(PB)]
        for i, q in enumerate(qs):
            for copy in copies(q, i):
                copy.start()
        for i, q in enumerate(qs):
            for copy in copies(q, i):
                copy.wait()
        for i in range(0, PB, 2):
            two_pairs(
                lane, x, i,
                [lambda g, k=k: temps[k, pl.ds(g * 8, 8), :] for k in (i, i + 1)],
                [lambda g, c, k=k: spec[k, c, :, pl.ds(g * 128, 128)] for k in (i, i + 1)],
            )
        y[...] = mm(x[...], inv_ref[...])
        for i in range(PB):
            add(first + i, y[pl.ds(i * 8, 8), :] * rs[i], sums[0])

    def late(n, carry):
        first = PAIRS + n * PB

        @pl.when(order_ref[0, first] >= 0)
        def _():
            late_block(first)

        return carry

    @pl.when(order_ref[0, PAIRS] >= 0)
    def _():
        lax.fori_loop(0, (PLACES - PAIRS) // PB, late, 0)

    same = (pt_ref[...] == lax.broadcasted_iota(jnp.int32, (T_DEV, PAIRS), 0)) & (
        lax.broadcasted_iota(jnp.int32, (T_DEV, PAIRS), 1) < live
    )
    counts = jnp.sum(same.astype(jnp.float32), axis=1, keepdims=True)
    scale = jnp.sqrt(SCALE / counts)
    sum0[...] = (sum0[...] + sum1[...]) + (sum2[...] + sum3[...])
    for g in range(4):
        lanes = pl.ds(g * 128, 128)
        head_ref[:, lanes] = sum0[pl.ds(g * 8, T_DEV, stride=64), :] * scale
        for h in range(8):
            v = sum0[pl.ds(32 + g * 8 + h, T_DEV, stride=64), :]
            if h < 7:
                v = v + sum0[pl.ds(g * 8 + h + 1, T_DEV, stride=64), :]
            out_ref[h, :, lanes] = v * scale


def pair_call(order, slot, tmpl, off, live, inverse, spec, rs, t, done):
    smem = pl.BlockSpec(memory_space=pltpu.SMEM)
    vmem = pl.BlockSpec(memory_space=pltpu.VMEM)
    hbm = pl.BlockSpec(memory_space=pl.ANY)
    f32, bf16 = jnp.float32, jnp.bfloat16
    return pl.pallas_call(
        pair_kernel,
        out_shape=[jax.ShapeDtypeStruct((8, T_DEV, TL), f32), jax.ShapeDtypeStruct((T_DEV, TL), f32)],
        in_specs=[smem] * 5 + [vmem] * 2 + [hbm] * 4,
        out_specs=[vmem] * 2,
        scratch_shapes=[
        ]
        + [pltpu.VMEM(((T_DEV + 1) * 64, 128), f32)] * SUMS
        + [
            pltpu.VMEM((PAIRS, 8, TL), f32),
            pltpu.VMEM((PB * 8, NBINS), bf16),
            pltpu.VMEM((PB * 8, TL), f32),
            pltpu.VMEM((PB, 3, 16, TL), bf16),
            pltpu.VMEM((PB, 8, TL), f32),
            pltpu.VMEM((PB, 32, 128), f32),
            pltpu.SemaphoreType.DMA((CHUNKS,)),
            pltpu.SemaphoreType.DMA((PB,)),
            pltpu.SemaphoreType.DMA((PB,)),
            pltpu.SemaphoreType.DMA((PB,)),
        ],
        compiler_params=pltpu.CompilerParams(vmem_limit_bytes=60 * 2**20),
        name="pairs",
    )(order, slot, tmpl, off, live, inverse, tmpl.reshape(1, PAIRS), spec, rs, t, done)


def shards(mesh, records, templates, requests, pair_slot, pair_template, pair_offset, live_pairs):
    count, depth = mesh.shape["tmpl"], mesh.shape["sta"]
    rec = jnp.transpose(records, (0, 2, 1, 3)).reshape(24, 32, TL)
    ask = jnp.transpose(requests.reshape(count, FETCH))
    spec, rs, temps, done, order = exchange_call(
        mesh, pair_slot, rec, ask, jnp.transpose(templates, (1, 0, 2)), jnp.asarray(FORWARD),
        jnp.asarray(INVERSE), live_pairs,
    )
    out, head = pair_call(
        order, pair_slot, pair_template, pair_offset, live_pairs, jnp.asarray(INVERSE), spec, rs, temps, done
    )
    head = lax.ppermute(head, "sta", [(i, i - 1) for i in range(1, depth)])
    return out.at[7].add(head)


def solution(mesh):
    in_specs = (
        P("sta", "tmpl", None, None),
        P("tmpl", None, None),
        P("tmpl", None, None),
        P("tmpl"),
        P("tmpl"),
        P("tmpl"),
        P("tmpl"),
    )
    return jax.shard_map(
        functools.partial(shards, mesh), mesh=mesh, in_specs=in_specs,
        out_specs=P("sta", "tmpl", None), check_vma=False,
    )
```

```python
import functools

import jax
import jax.numpy as jnp
import numpy as np
from jax import lax
from jax.experimental import pallas as pl
from jax.experimental.pallas import tpu as pltpu
from jax.sharding import PartitionSpec as P

TL = 512
NBINS = 2 * TL
T_DEV = 32
FETCH = 4
SCALE = 3.0 * TL
EPSILON = 1e-05
MESH = pl.DeviceIdType.MESH
PB = 16
PAIRS = 512
PLACES = 1024


def dft_tables():
    n = np.arange(TL)[:, None]
    k = np.arange(TL)[None, :]
    angles = (n * k % NBINS) * (2.0 * np.pi / NBINS)
    parity = np.where(n % 2 == 0, 1.0, -1.0)
    second = np.where(k == 0, parity, -np.sin(angles))
    forward = np.concatenate([np.cos(angles), second], axis=1).astype(jnp.bfloat16)
    alternate = np.where(k % 2 == 0, 1.0, -1.0)
    cosine_rows = np.where(n == 0, 1.0, 2.0 * np.cos(angles)) / NBINS
    sine_rows = np.where(n == 0, alternate, -2.0 * np.sin(angles)) / NBINS
    inverse = np.concatenate([cosine_rows, sine_rows], axis=0).astype(jnp.bfloat16)
    return forward, inverse


FORWARD, INVERSE = dft_tables()

GROUPS = 8
PER = 4
ROWS = FETCH * 24


def split(value):
    high = value.astype(jnp.bfloat16)
    low = (value - high.astype(jnp.float32)).astype(jnp.bfloat16)
    return high, low


def mm(left, right):
    return jnp.dot(left, right, preferred_element_type=jnp.float32)


def cross_terms(lane, group, template, station):
    real = imag = None
    for c in range(3):
        rows = station(c).astype(jnp.float32)
        br, bm = rows[:8], rows[8:]
        ar = jnp.broadcast_to(template[c:c + 1], (8, 128))
        am = jnp.broadcast_to(template[c + 3:c + 4], (8, 128))
        cr = ar
        if group == 0:
            cr = jnp.where(lane == 0, am, ar)
            am = jnp.where(lane == 0, 0.0, am)
        r = ar * br + am * bm
        m = cr * bm - am * br
        real = r if real is None else real + r
        imag = m if imag is None else imag + m
    return real, imag


def two_pairs(lane, x, i, templates, stations):
    for g in range(4):
        terms = [cross_terms(lane, g, t(g), functools.partial(s, g)) for t, s in zip(templates, stations)]
        for half in range(2):
            rows = jnp.concatenate([t[half] for t in terms], axis=0).astype(jnp.bfloat16)
            x[pl.ds(i * 8, 16), pl.ds(half * TL + g * 128, 128)] = rows


def exchange_kernel(
    count, depth, slot_s, rec_ref, ask_ref, tmp_ref, fwd_ref, inv_ref, slot_ref, tmpl_ref, off_ref, live_s,
    spec_out, rs_out, t_out, done_out, order_out, codes_out,
    rec32, asks, asked, wanted, send, recv, halo_send, halo_recv, parts, part_energy, halo_spec,
    spec, rs, temps, order, codes, order_s, x0, x1, done,
    ask_send_sem, ask_recv_sem, send_sem, recv_sem, halo_send_sem, halo_recv_sem, local_sem, done_sem, spec_sem, rs_sem,
):
    me = lax.axis_index("tmpl")
    z = lax.axis_index("sta")
    above = lax.rem(z + 1, depth)
    below = lax.rem(z + depth - 1, depth)

    y, x, core = me // 8, lax.rem(me // 2, 4), lax.rem(me, 2)

    def place(up, right, other):
        return lax.rem(y + up + 8, 4) * 8 + lax.rem(x + right + 8, 4) * 2 + lax.rem(core + other, 2)

    def steps(i):
        return lax.rem(i // 4, 4), lax.rem(i, 4), i // 16

    def ahead(i):
        up, right, other = steps(i)
        return place(up, right, other)

    def behind(i):
        up, right, other = steps(i)
        return place(-up, -right, other)

    barrier = pltpu.get_barrier_semaphore()

    def greet(i, carry):
        pl.semaphore_signal(barrier, inc=1, device_id={"tmpl": ahead(i)}, device_id_type=MESH)
        return carry

    lax.fori_loop(1, count, greet, 0)
    pl.semaphore_signal(barrier, inc=1, device_id={"sta": above}, device_id_type=MESH)
    pl.semaphore_signal(barrier, inc=1, device_id={"sta": below}, device_id_type=MESH)

    def widen(i, carry):
        block = rec_ref[i].astype(jnp.float32)
        for g in range(4):
            rec32[g, pl.ds(pl.multiple_of(i * 32, 32), 32), :] = block[:, g * 128:(g + 1) * 128]
        return carry

    lax.fori_loop(0, 24, widen, 0)
    rows = lax.broadcasted_iota(jnp.int32, (count, count), 0)
    lanes = lax.broadcasted_iota(jnp.int32, (count, count), 1)
    table = jnp.zeros((count, 128), jnp.int32)
    for f in range(FETCH):
        column = jnp.sum(jnp.where(rows == lanes, ask_ref[f:f + 1, :], 0), axis=1, keepdims=True)
        table = jnp.where(lax.broadcasted_iota(jnp.int32, (count, 128), 1) == f, column, table)
    for d in range(count):
        asks[d] = table[d:d + 1, :]
    pl.semaphore_wait(barrier, count + 1)

    def ask_copy(i):
        return pltpu.make_async_remote_copy(
            src_ref=asks.at[ahead(i)], dst_ref=asked.at[i],
            send_sem=ask_send_sem.at[i], recv_sem=ask_recv_sem.at[i],
            device_id={"tmpl": ahead(i)}, device_id_type=MESH,
        )

    def ask_start(i, carry):
        ask_copy(i).start()
        return carry

    lax.fori_loop(1, count, ask_start, 0)
    asked[0] = asks[me]

    lane = lax.broadcasted_iota(jnp.int32, (128, 128), 1)

    def template_block(n, carry):
        first = pl.multiple_of(n * 128, 128)
        pieces = [tmp_ref[c, pl.ds(first, 128), :] for c in range(3)]
        energy = sum(jnp.sum(jnp.square(p.astype(jnp.float32)), axis=1, keepdims=True) for p in pieces)
        factor = lax.rsqrt(energy / SCALE + EPSILON) / SCALE
        for c in range(3):
            found = mm(pieces[c], fwd_ref[...]) * factor
            for g in range(4):
                base = n * 4096 + g * 8
                temps[pl.ds(base + c, 128, stride=32), :] = found[:, g * 128:(g + 1) * 128]
                temps[pl.ds(base + c + 3, 128, stride=32), :] = found[:, TL + g * 128:TL + (g + 1) * 128]
        return carry

    def ask_wait(i, carry):
        ask_copy(i).wait()
        return carry

    f32, bf16 = jnp.float32, jnp.bfloat16
    i32 = jnp.int32
    live = live_s[0]
    pair_row = lax.broadcasted_iota(i32, (PAIRS, PAIRS), 1)
    pair_col = lax.broadcasted_iota(i32, (PAIRS, PAIRS), 0)
    source = lax.shift_right_logical(slot_ref[...], 2)
    key_row = ((source + me) & 1) * 4 + ((lax.shift_right_logical(source, 3) - y) & 3)
    key_row = jnp.where(pair_row[:1] < live, key_row, GROUPS)
    key_col = jnp.sum(jnp.where(pair_row == pair_col, key_row, 0), axis=1, keepdims=True)
    ahead_of = (key_row < key_col) | ((key_row == key_col) & (pair_row < pair_col))
    rank_col = jnp.sum(ahead_of.astype(i32), axis=1, keepdims=True)
    group_row = lax.broadcasted_iota(i32, (PAIRS, 128), 1)
    below_count = jnp.sum((key_col < group_row).astype(i32), axis=0, keepdims=True)
    gap = jnp.maximum(64 * group_row[:1] - 32, 0) - below_count
    gap = jnp.where((group_row <= key_col) & (group_row < GROUPS), gap, 0)
    code_row = (tmpl_ref[...] * 64 + 24 - 8 * lax.shift_right_logical(off_ref[...], 7)) * 128 + (off_ref[...] & 127)
    code_col = jnp.sum(jnp.where(pair_row == pair_col, code_row, 0), axis=1, keepdims=True)
    place_col = rank_col + jnp.max(gap, axis=1, keepdims=True)
    place_col = jnp.where(key_col < GROUPS, place_col, 2 * PLACES)
    for n in range(PLACES // 128):
        here = place_col == group_row + n * 128
        found = jnp.sum(jnp.where(here, pair_col[:, :128] + 1, 0), axis=0, keepdims=True)
        order[:, pl.ds(n * 128, 128)] = found - 1
        code = jnp.sum(jnp.where(here, code_col, 0), axis=0, keepdims=True)
        codes[:, pl.ds(n * 128, 128)] = jnp.where(found > 0, code, (T_DEV * 64 + 24) * 128)
    order_copies = (
        pltpu.make_async_copy(order, order_s, local_sem.at[4]),
        pltpu.make_async_copy(order, order_out, local_sem.at[2]),
        pltpu.make_async_copy(codes, codes_out, local_sem.at[5]),
    )
    for copy in order_copies:
        copy.start()
    lax.fori_loop(0, 2, template_block, 0)
    lax.fori_loop(1, count, ask_wait, 0)
    to_scalar = pltpu.make_async_copy(asked, wanted, local_sem.at[0])
    to_scalar.start()
    to_scalar.wait()

    def gather(i):
        rows = []
        for f in range(FETCH):
            s = wanted[i, 0, f]
            for c in range(3):
                rows.append(
                    jnp.concatenate(
                        [rec32[g, pl.ds(c * 32 + s, 8, stride=96), :] for g in range(4)], axis=1
                    )
                )
        return jnp.concatenate(rows, axis=0).astype(jnp.bfloat16)

    def data_copy(i):
        return pltpu.make_async_remote_copy(
            src_ref=send.at[i], dst_ref=recv.at[i],
            send_sem=send_sem.at[i], recv_sem=recv_sem.at[i],
            device_id={"tmpl": behind(i)}, device_id_type=MESH,
        )

    def data_start(i, carry):
        send[i] = gather(i)
        data_copy(i).start()
        return carry

    lax.fori_loop(1, count, data_start, 0)
    recv[0] = gather(0)

    for copy in order_copies:
        copy.wait()
    lax.fori_loop(2, 4, template_block, 0)
    out_t = pltpu.make_async_copy(temps, t_out, local_sem.at[1])
    out_t.start()

    x1[...] = jnp.zeros_like(x1)
    lane8 = lax.broadcasted_iota(jnp.int32, (8, 128), 1)

    def pair_at(place):
        return jnp.maximum(order_s[0, jnp.maximum(place, 0)], 0)

    def cross_block(block, x):
        for i in range(0, PB, 2):
            templates, stations = [], []
            for k in range(2):
                q = pair_at(block * PB + i + k)
                base = slot_s[q] * 3
                templates.append(
                    lambda g, q=q: temps[pl.ds(q * 32 + g * 8, 8), :]
                )
                stations.append(lambda g, c, base=base: spec[base + c, :, pl.ds(g * 128, 128)])
            two_pairs(lane8, x, i, templates, stations)

    def invert_block(block, x):
        lagged = mm(x[...], inv_ref[...])
        for i in range(PB):
            place = block * PB + i
            done[place + PB] = lagged[i * 8:i * 8 + 8] * rs[slot_s[pair_at(place)]]

    def done_copy(n):
        rows = pl.ds(n * 32, 32)
        return pltpu.make_async_copy(done.at[rows], done_out.at[rows], done_sem.at[n])

    def pair_turn(n, carry):
        invert_block(2 * n - 1, x1)
        cross_block(2 * n, x0)
        invert_block(2 * n, x0)
        cross_block(2 * n + 1, x1)
        done_copy(n).start()
        return carry

    def stage(k):
        lax.fori_loop(jnp.maximum(2 * k - 1, 0), 2 * k + 1, pair_turn, 0)

    row = lax.broadcasted_iota(jnp.int32, (48, PER * ROWS), 0)
    col = lax.broadcasted_iota(jnp.int32, (48, PER * ROWS), 1)
    pick = (col == (row % 16) * 24 + (row // 16) * 8).astype(jnp.bfloat16)
    sample = lax.broadcasted_iota(jnp.int32, (TL, TL), 0)
    lag = lax.broadcasted_iota(jnp.int32, (TL, TL), 1)
    later = (sample >= lag).astype(jnp.bfloat16)
    earlier = (sample < lag).astype(jnp.bfloat16)
    last = lax.broadcasted_iota(jnp.int32, (8, 128), 0) == 7
    odd = jnp.where(lax.broadcasted_iota(jnp.int32, (8, 128), 1) % 2 == 0, 1.0, -1.0)

    def halo_copy(g):
        return pltpu.make_async_remote_copy(
            src_ref=halo_send.at[g], dst_ref=halo_recv.at[g],
            send_sem=halo_send_sem.at[g], recv_sem=halo_recv_sem.at[g],
            device_id={"sta": below}, device_id_type=MESH,
        )

    def main_part(g, slot):
        for k in range(PER):
            i = g * PER + k

            @pl.when(i > 0)
            def _():
                data_copy(i).wait_recv()

        block = recv[pl.ds(g * PER, PER)].reshape(PER * ROWS, TL)
        halo_send[g] = mm(pick, block).astype(jnp.bfloat16)
        halo_copy(g).start()
        for n in range(4):
            columns = pl.ds(n * 256, 256)
            parts[slot, :, columns] = mm(block, fwd_ref[:, columns])
        squares = jnp.square(block.astype(jnp.float32)).reshape(16, 3, 8, TL)
        squares = (squares[:, 0] + squares[:, 1] + squares[:, 2]).reshape(128, TL)
        high, low = split(squares)
        part_energy[slot, 0] = mm(high, later) + mm(low, later)
        part_energy[slot, 1] = mm(high, earlier) + mm(low, earlier)

    def station_at(g, s):
        return ahead(g * PER + s // FETCH) * FETCH + lax.rem(s, FETCH)

    def halo_part(g, slot):
        halo_copy(g).wait_recv()
        block = jnp.where(z == depth - 1, jnp.zeros((48, TL), jnp.bfloat16), halo_recv[g])
        found = mm(block, fwd_ref[...])
        for n in range(8):
            halo_spec[n, 0:48, :] = found[:, n * 128:(n + 1) * 128]
        squares = jnp.square(block.astype(jnp.float32))
        high, low = split(squares[0:16] + squares[16:32] + squares[32:48])
        energy = mm(high, earlier) + mm(low, earlier)
        for n in range(4):
            halo_spec[n, 48:64, :] = energy[:, n * 128:(n + 1) * 128]

        def station(s, carry):
            for c in range(3):
                base = pl.multiple_of(s * 24 + c * 8, 8)
                halves = []
                for n in range(8):
                    now = parts[slot, pl.ds(base, 8), pl.ds(n * 128, 128)]
                    beyond = halo_spec[n, pl.ds(c * 16 + s, 8, stride=0), :]
                    following = jnp.where(last, beyond, pltpu.roll(now, 7, 0))
                    halves.append(now + odd * following)
                real = jnp.concatenate(halves[:4], axis=1)
                imag = jnp.concatenate(halves[4:], axis=1)
                spec[station_at(g, s) * 3 + c] = jnp.concatenate([real, imag], axis=0).astype(jnp.bfloat16)
            base = pl.multiple_of(s * 8, 8)
            for n in range(4):
                columns = pl.ds(n * 128, 128)
                early = part_energy[slot, 1, pl.ds(base, 8), columns]
                beyond = halo_spec[n, pl.ds(48 + s, 8, stride=0), :]
                early = jnp.where(last, beyond, pltpu.roll(early, 7, 0))
                total = part_energy[slot, 0, pl.ds(base, 8), columns] + early
                rs[station_at(g, s), :, columns] = lax.rsqrt(total / SCALE + EPSILON)
            return carry

        lax.fori_loop(0, 16, station, 0, unroll=2)

        def leave(k, carry):
            spec_copy(g * PER + k).start()
            rs_copy(g * PER + k).start()
            return carry

        lax.fori_loop(0, PER, leave, 0)

    def spec_copy(i):
        rows = pl.ds(ahead(i) * (FETCH * 3), FETCH * 3)
        return pltpu.make_async_copy(spec.at[rows], spec_out.at[rows], spec_sem.at[i])

    def rs_copy(i):
        rows = pl.ds(ahead(i) * FETCH, FETCH)
        return pltpu.make_async_copy(rs.at[rows], rs_out.at[rows], rs_sem.at[i])

    main_part(0, 0)

    def turn(g, carry):
        main_part(g, lax.rem(g, 2))
        halo_part(g - 1, lax.rem(g - 1, 2))
        stage(g - 1)
        return carry

    lax.fori_loop(1, GROUPS, turn, 0)
    halo_part(GROUPS - 1, (GROUPS - 1) % 2)
    lax.fori_loop(2 * GROUPS - 3, PAIRS // 32, pair_turn, 0)
    invert_block(PAIRS // PB - 1, x1)
    rest = pltpu.make_async_copy(done.at[pl.ds(PAIRS, PB)], done_out.at[pl.ds(PAIRS, PB)], local_sem.at[3])
    rest.start()

    def finish(i, carry):
        data_copy(i).wait_send()
        return carry

    lax.fori_loop(1, count, finish, 0)

    def finish_group(g, carry):
        halo_copy(g).wait_send()
        return carry

    def finish_source(i, carry):
        spec_copy(i).wait()
        rs_copy(i).wait()
        return carry

    def finish_places(n, carry):
        done_copy(n).wait()
        return carry

    lax.fori_loop(0, GROUPS, finish_group, 0)
    lax.fori_loop(0, count, finish_source, 0)
    lax.fori_loop(0, PAIRS // 32, finish_places, 0)
    rest.wait()
    out_t.wait()


def exchange_call(mesh, slot, rec, ask, templates, forward, inverse, tmpl, off, live):
    count, depth = mesh.shape["tmpl"], mesh.shape["sta"]
    vmem = pl.BlockSpec(memory_space=pltpu.VMEM)
    hbm = pl.BlockSpec(memory_space=pl.ANY)
    smem = pl.BlockSpec(memory_space=pltpu.SMEM)
    f32, bf16 = jnp.float32, jnp.bfloat16
    slots = count * FETCH
    return pl.pallas_call(
        functools.partial(exchange_kernel, count, depth),
        out_shape=[
            jax.ShapeDtypeStruct((slots * 3, 16, TL), bf16),
            jax.ShapeDtypeStruct((slots, 8, TL), f32),
            jax.ShapeDtypeStruct((512 * 32, 128), f32),
            jax.ShapeDtypeStruct((PAIRS + PB, 8, TL), f32),
            jax.ShapeDtypeStruct((1, PLACES), jnp.int32),
            jax.ShapeDtypeStruct((1, PLACES), jnp.int32),
        ],
        in_specs=[smem] + [vmem] * 8 + [smem],
        out_specs=[hbm] * 6,
        scratch_shapes=[
            pltpu.VMEM((4, 768, 128), f32),
            pltpu.VMEM((count, 1, 128), jnp.int32),
            pltpu.VMEM((count, 1, 128), jnp.int32),
            pltpu.SMEM((count, 1, 128), jnp.int32),
            pltpu.VMEM((count, ROWS, TL), bf16),
            pltpu.VMEM((count, ROWS, TL), bf16),
            pltpu.VMEM((GROUPS, 48, TL), bf16),
            pltpu.VMEM((GROUPS, 48, TL), bf16),
            pltpu.VMEM((2, PER * ROWS, NBINS), f32),
            pltpu.VMEM((2, 2, 128, TL), f32),
            pltpu.VMEM((8, 64, 128), f32),
            pltpu.VMEM((slots * 3, 16, TL), bf16),
            pltpu.VMEM((slots, 8, TL), f32),
            pltpu.VMEM((512 * 32, 128), f32),
            pltpu.VMEM((1, PLACES), jnp.int32),
            pltpu.VMEM((1, PLACES), jnp.int32),
            pltpu.SMEM((1, PLACES), jnp.int32),
            pltpu.VMEM((PB * 8, NBINS), bf16),
            pltpu.VMEM((PB * 8, NBINS), bf16),
            pltpu.VMEM((PAIRS + PB, 8, TL), f32),
            pltpu.SemaphoreType.DMA((count,)),
            pltpu.SemaphoreType.DMA((count,)),
            pltpu.SemaphoreType.DMA((count,)),
            pltpu.SemaphoreType.DMA((count,)),
            pltpu.SemaphoreType.DMA((GROUPS,)),
            pltpu.SemaphoreType.DMA((GROUPS,)),
            pltpu.SemaphoreType.DMA((6,)),
            pltpu.SemaphoreType.DMA((PAIRS // 32,)),
            pltpu.SemaphoreType.DMA((count,)),
            pltpu.SemaphoreType.DMA((count,)),
        ],
        compiler_params=pltpu.CompilerParams(
            collective_id=0, has_side_effects=True, vmem_limit_bytes=60 * 2**20
        ),
        name="exchange",
    )(
        slot, rec, ask, templates, forward, inverse, slot.reshape(1, PAIRS), tmpl.reshape(1, PAIRS),
        off.reshape(1, PAIRS), live,
    )


SUMS = 4
CHUNKS = 8


def pair_kernel(
    order_ref, codes_ref, slot_ref, live_ref, pt_ref, inv_in, spec_in, rs_in, t_in, done_in,
    out_ref, head_ref,
    sum0, sum1, sum2, sum3, done, x, y, spec, rs, temps, inv_ref, inv_sem, done_sem, spec_sem, rs_sem, t_sem,
):
    live = live_ref[0]
    lane = lax.broadcasted_iota(jnp.int32, (8, 128), 1)

    def chunk(n):
        rows = pl.ds(n * (PAIRS // CHUNKS), PAIRS // CHUNKS)
        return pltpu.make_async_copy(
            done_in.at[pl.ds(n * (PAIRS // CHUNKS) + PB, PAIRS // CHUNKS)], done.at[rows], done_sem.at[n]
        )

    for n in range(CHUNKS):
        chunk(n).start()
    sums = (sum0, sum1, sum2, sum3)
    for acc in sums:
        acc[...] = jnp.zeros_like(acc)

    def add(place, row, acc):
        code = codes_ref[0, place]
        fine = code & 127
        low = lane < 128 - fine
        turned = [pltpu.roll(row[:, g * 128:(g + 1) * 128], 128 - fine, 1) for g in range(4)]
        parts = [jnp.where(low, 0.0, turned[0])]
        for g in range(3):
            parts.append(jnp.where(low, turned[g], turned[g + 1]))
        parts.append(jnp.where(low, turned[3], 0.0))
        base = pl.multiple_of(lax.shift_right_logical(code, 7), 8)
        acc[pl.ds(base, 40), :] += jnp.concatenate(parts, axis=0)

    def add_some(b, carry):
        for i in range(16):
            add(b * 16 + i, done[b * 16 + i], sums[i % SUMS])
        return carry

    for n in range(CHUNKS):
        chunk(n).wait()
        lax.fori_loop(n * (PAIRS // CHUNKS // 16), (n + 1) * (PAIRS // CHUNKS // 16), add_some, 0)

    def copies(q, i):
        s = slot_ref[q]
        return (
            pltpu.make_async_copy(spec_in.at[pl.ds(s * 3, 3)], spec.at[i], spec_sem.at[i]),
            pltpu.make_async_copy(rs_in.at[s], rs.at[i], rs_sem.at[i]),
            pltpu.make_async_copy(t_in.at[pl.ds(pl.multiple_of(q * 32, 32), 32)], temps.at[i], t_sem.at[i]),
        )

    def late_block(first):
        qs = [jnp.maximum(order_ref[0, first + i], 0) for i in range(PB)]
        for i, q in enumerate(qs):
            for copy in copies(q, i):
                copy.start()
        for i, q in enumerate(qs):
            for copy in copies(q, i):
                copy.wait()
        for i in range(0, PB, 2):
            two_pairs(
                lane, x, i,
                [lambda g, k=k: temps[k, pl.ds(g * 8, 8), :] for k in (i, i + 1)],
                [lambda g, c, k=k: spec[k, c, :, pl.ds(g * 128, 128)] for k in (i, i + 1)],
            )
        y[...] = mm(x[...], inv_ref[...])
        for i in range(PB):
            add(first + i, y[pl.ds(i * 8, 8), :] * rs[i], sums[0])

    def late(n, carry):
        first = PAIRS + n * PB

        @pl.when(order_ref[0, first] >= 0)
        def _():
            late_block(first)

        return carry

    @pl.when(order_ref[0, PAIRS] >= 0)
    def _():
        table = pltpu.make_async_copy(inv_in, inv_ref, inv_sem)
        table.start()
        table.wait()
        lax.fori_loop(0, (PLACES - PAIRS) // PB, late, 0)

    same = (pt_ref[...] == lax.broadcasted_iota(jnp.int32, (T_DEV, PAIRS), 0)) & (
        lax.broadcasted_iota(jnp.int32, (T_DEV, PAIRS), 1) < live
    )
    counts = jnp.sum(same.astype(jnp.float32), axis=1, keepdims=True)
    scale = jnp.sqrt(SCALE / counts)
    sum0[...] = (sum0[...] + sum1[...]) + (sum2[...] + sum3[...])
    for g in range(4):
        lanes = pl.ds(g * 128, 128)
        head_ref[:, lanes] = sum0[pl.ds(g * 8, T_DEV, stride=64), :] * scale
        for h in range(8):
            v = sum0[pl.ds(32 + g * 8 + h, T_DEV, stride=64), :]
            if h < 7:
                v = v + sum0[pl.ds(g * 8 + h + 1, T_DEV, stride=64), :]
            out_ref[h, :, lanes] = v * scale


def pair_call(order, codes, slot, tmpl, live, inverse, spec, rs, t, done):
    smem = pl.BlockSpec(memory_space=pltpu.SMEM)
    vmem = pl.BlockSpec(memory_space=pltpu.VMEM)
    hbm = pl.BlockSpec(memory_space=pl.ANY)
    f32, bf16 = jnp.float32, jnp.bfloat16
    return pl.pallas_call(
        pair_kernel,
        out_shape=[jax.ShapeDtypeStruct((8, T_DEV, TL), f32), jax.ShapeDtypeStruct((T_DEV, TL), f32)],
        in_specs=[smem] * 4 + [vmem] + [hbm] * 5,
        out_specs=[vmem] * 2,
        scratch_shapes=[
        ]
        + [pltpu.VMEM(((T_DEV + 1) * 64, 128), f32)] * SUMS
        + [
            pltpu.VMEM((PAIRS, 8, TL), f32),
            pltpu.VMEM((PB * 8, NBINS), bf16),
            pltpu.VMEM((PB * 8, TL), f32),
            pltpu.VMEM((PB, 3, 16, TL), bf16),
            pltpu.VMEM((PB, 8, TL), f32),
            pltpu.VMEM((PB, 32, 128), f32),
            pltpu.VMEM((NBINS, TL), bf16),
            pltpu.SemaphoreType.DMA,
            pltpu.SemaphoreType.DMA((CHUNKS,)),
            pltpu.SemaphoreType.DMA((PB,)),
            pltpu.SemaphoreType.DMA((PB,)),
            pltpu.SemaphoreType.DMA((PB,)),
        ],
        compiler_params=pltpu.CompilerParams(vmem_limit_bytes=60 * 2**20),
        name="pairs",
    )(order, codes, slot, live, tmpl.reshape(1, PAIRS), inverse, spec, rs, t, done)


def shards(mesh, records, templates, requests, pair_slot, pair_template, pair_offset, live_pairs):
    count, depth = mesh.shape["tmpl"], mesh.shape["sta"]
    rec = jnp.transpose(records, (0, 2, 1, 3)).reshape(24, 32, TL)
    ask = jnp.transpose(requests.reshape(count, FETCH))
    spec, rs, temps, done, order, codes = exchange_call(
        mesh, pair_slot, rec, ask, jnp.transpose(templates, (1, 0, 2)), jnp.asarray(FORWARD),
        jnp.asarray(INVERSE), pair_template, pair_offset, live_pairs,
    )
    out, head = pair_call(
        order, codes, pair_slot, pair_template, live_pairs, jnp.asarray(INVERSE), spec, rs, temps, done
    )
    head = lax.ppermute(head, "sta", [(i, i - 1) for i in range(1, depth)])
    return out.at[7].add(head)


def solution(mesh):
    in_specs = (
        P("sta", "tmpl", None, None),
        P("tmpl", None, None),
        P("tmpl", None, None),
        P("tmpl"),
        P("tmpl"),
        P("tmpl"),
        P("tmpl"),
    )
    return jax.shard_map(
        functools.partial(shards, mesh), mesh=mesh, in_specs=in_specs,
        out_specs=P("sta", "tmpl", None), check_vma=False,
    )
```
